32 devices in a mesh: groups: 2 (over x), docs: 8 (over z, y), tensor: 2 (over core).
Axes of the slice: x: 2, y: 2, z: 4, core: 2. Of those that a mesh axis runs over, the one named last changes fastest.
Arguments:
- sample_act: bfloat16 [128, 32, 11008], P(('groups', 'docs'), None, 'tensor'), parts along dimension 0, may hold values from -6 to 6
- sample_grad: bfloat16 [128, 32, 4096], P(('groups', 'docs'), None, 'tensor'), parts along dimension 0, may hold values from -6 to 6
- doc_act: bfloat16 [16, 768, 11008], P(('groups', 'docs'), None, 'tensor'), parts along dimension 0, may hold values from -6 to 6
- doc_grad: bfloat16 [16, 768, 4096], P(('groups', 'docs'), None, 'tensor'), parts along dimension 0, may hold values from -6 to 6
- pair_doc: int32 [256, 1], P(('groups', 'docs')), parts along dimension 0, may hold values from 0 to 7; in each aligned block of 16 rows (0 to 15, 16 to 31, ...) at most 2 rows name the same one
- pair_sample: int32 [256], P(('groups', 'docs')), parts along dimension 0, may hold values from 0 to 7
Outputs:
- influence: float32 [256], P(('groups', 'docs')), parts along dimension 0
The draws below stay inside these ranges and needn't reach their ends.
There are 2 independent parts, one for each index of `groups`. The reference program is written for one: setup_inputs(seed, part) draws one part's arguments, and reference() takes and returns one part's arrays. A program takes and returns all parts, laid end to end along the dimension named above; each array names one. Nothing has to cross between parts.
Inputs may be any that keep to these rules, and one draw needn't show every extreme that they name: `pair_doc`: among the 16 pairs listed by one index of docs, no document is named more than 2 times, a bound that some block reaches; document d is owned by index d of docs. The sample of pair p is sample (p // 16) * 8 + pair_sample[p].
All inputs are finite; a program needn't handle non-finite values.
Results may differ from the reference program's by a relative error of at most 0.0003.
Values may be sent and summed in bfloat16 or wider, within the bound.
No kernel may reach another device: no remote copies, remote signals or barrier semaphores. Data moves between devices by JAX's collectives and lax.ppermute only.
A program may use at most 128 MiB of HBM per device.

```python
import math
import jax
import jax.numpy as jnp
import numpy as np
from jax import lax

FF = 11008
D = 4096
SEQ_S = 32
SEQ_D = 768
SAMP_DEV = 8
PAIRS_DEV = 16
CAP = 2
SAMPLES = 64
DOCS = 8
PAIRS = 128


def with_ends(drawn, stream_key, low, high):
    extent = drawn.shape
    place = [jax.random.randint(jax.random.fold_in(stream_key, axis), (), 0, extent[axis]) for axis in range(len(extent))]
    drawn = drawn.at[tuple(place)].set(low)
    longest = extent.index(max(extent))
    place[longest] = (place[longest] + 1) % extent[longest]
    return drawn.at[tuple(place)].set(high)


def block_scale(rng, extent, split, smallest, high):
    def one(dim, parts):
        draws = jax.random.uniform(jax.random.fold_in(jax.random.fold_in(rng, 6), dim), (parts,), jnp.float32, smallest / len(split), high / len(split))
        return jnp.repeat(jnp.exp(draws), extent[dim] // parts).reshape((-1,) + (1,) * (len(extent) - dim - 1))

    factor_of = one(*split[0])
    for cut in split[1:]:
        factor_of = factor_of * one(*cut)
    return factor_of


def routed_block(stream_key, own, number, rows, count, top, limit, lean):
    sequence = jax.random.permutation(stream_key, count)
    packed, common = load_shares(count, rows * top, limit, lean, True), load_shares(count, rows * top, limit, lean, False)
    places = jnp.arange(count)

    def named(lengths, rotation):
        used = int((lengths > 0).sum())
        fixed = max(1, used // 4)
        shifted = fixed + (places - fixed + rotation * (used - fixed)) % max(1, count - fixed)
        return jnp.zeros((count,), jnp.int32).at[sequence[jnp.where(places < fixed, places, shifted)]].set(jnp.asarray(lengths, jnp.int32))

    lengths = jnp.where(number % 4 == 0, named(packed, number // 4), named(common, number - number // 4 - 1))
    mixed = jax.random.permutation(jax.random.fold_in(own, 3), count)
    donor, receiver = mixed[0:count // 2 * 2:2], mixed[1:count // 2 * 2:2]
    room = jnp.minimum(lengths[donor] - 1, limit - lengths[receiver]) // 2
    room = jnp.where((donor == sequence[0]) | (receiver == sequence[0]) | (lengths[receiver] == 0), 0, jnp.maximum(room, 0))
    shifted = jax.random.randint(jax.random.fold_in(own, 4), (count // 2,), 0, 1 << 20) % (room + 1)
    lengths = lengths.at[donor].add(-shifted).at[receiver].add(shifted)
    labels = jnp.searchsorted(jnp.cumsum(lengths), jnp.arange(rows * top), side="right").astype(jnp.int32)
    table = labels.reshape(top, rows).T
    table = table[jax.random.permutation(jax.random.fold_in(own, 1), rows)]
    rotation = jax.random.randint(jax.random.fold_in(own, 2), (rows, 1), 0, top)
    return jnp.take_along_axis(table, (jnp.arange(top)[None, :] + rotation) % top, axis=1)


def load_shares(count, total, limit, lean, full):
    loads = [(1 << 20) // math.isqrt(standing ** lean) + 1 for standing in range(1, count + 1)]
    largest = limit if full else min(limit, max(-(-total // count), total * loads[0] // sum(loads)))
    least = 1 if total - largest >= count - 1 else 0
    given, spare = [largest] + [least] * (count - 1), total - largest - least * (count - 1)
    while spare > 0:
        free = [i for i in range(1, count) if given[i] < largest] or [i for i in range(1, count) if given[i] < limit]
        whole, remaining = sum([loads[i] for i in free]), spare
        for i in free:
            extra = min(limit - given[i], max(1, remaining * loads[i] // whole), spare)
            given[i] = given[i] + extra
            spare = spare - extra
    return np.array(given)


def normal_values(rng, dims, width, limit, pieces=(), dtype=jnp.bfloat16):
    values = jax.random.normal(rng, dims, jnp.float32) * width
    if len(pieces) > 0:
        values = block_scale(rng, dims, pieces, -0.22, 0.18) * values
    return jnp.clip(values, min=-limit, max=limit).astype(dtype)


def setup_inputs(seed: int = 0, part: int = 0) -> dict:
    key_of = jax.random.split(jax.random.key(seed), 7)
    part_splits = jax.random.split(jax.random.fold_in(key_of[6], part), 7)
    sample_act = normal_values(part_splits[0], (SAMPLES, SEQ_S, FF), 1.0, 6.0, ((0, 8), (2, 2)))
    sample_grad = normal_values(part_splits[1], (SAMPLES, SEQ_S, D), 1.0, 6.0, ((0, 8), (2, 2)))
    doc_act = normal_values(part_splits[2], (DOCS, SEQ_D, FF), 1.0, 6.0, ((0, 8), (2, 2)))
    doc_grad = normal_values(part_splits[3], (DOCS, SEQ_D, D), 1.0, 6.0, ((0, 8), (2, 2)))
    pair_doc_keys = jax.random.split(jax.random.fold_in(part_splits[4], 1), PAIRS // PAIRS_DEV)
    pair_doc_turns = jax.random.permutation(jax.random.fold_in(part_splits[4], 3), PAIRS // PAIRS_DEV)
    pair_doc = jax.vmap(lambda own, number: routed_block(jax.random.fold_in(part_splits[4], 2), own, number, PAIRS_DEV, DOCS, 1, CAP, 2))(pair_doc_keys, pair_doc_turns).reshape((PAIRS, 1))
    pair_sample = with_ends(jax.random.randint(part_splits[5], (PAIRS,), 0, SAMP_DEV), jax.random.fold_in(part_splits[5], 1), 0, SAMP_DEV - 1).astype(jnp.int32)
    return dict(sample_act=sample_act, sample_grad=sample_grad, doc_act=doc_act, doc_grad=doc_grad, pair_doc=pair_doc, pair_sample=pair_sample)


def reference(sample_act, sample_grad, doc_act, doc_grad, pair_doc, pair_sample):
    owner = (jnp.arange(PAIRS) // PAIRS_DEV).astype(jnp.int32)
    sample_ids = (owner * SAMP_DEV + pair_sample).astype(jnp.int32)
    doc_ids = pair_doc[:, 0].astype(jnp.int32)
    factor = 1.0 / jnp.sqrt(jnp.float32(FF) * jnp.float32(D) * jnp.float32(SEQ_S) * jnp.float32(SEQ_D))

    def one_pair(ids):
        sample_id, doc_id = ids
        act_gram = jnp.dot(sample_act[sample_id], doc_act[doc_id].T, preferred_element_type=jnp.float32)
        grad_gram = jnp.dot(sample_grad[sample_id], doc_grad[doc_id].T, preferred_element_type=jnp.float32)
        return jnp.sum(act_gram * grad_gram) * factor
    return lax.map(one_pair, (sample_ids, doc_ids))
```

```python
import functools

import jax
import jax.numpy as jnp
from jax import lax
from jax.experimental import pallas as pl
from jax.experimental.pallas import tpu as pltpu
from jax.sharding import PartitionSpec as P

FF = 11008
D = 4096
SEQ_S = 32
SEQ_D = 768
CAP = 2

ANY = pl.BlockSpec(memory_space=pl.ANY)
SMEM = pl.BlockSpec(memory_space=pltpu.SMEM)
VMEM = pl.BlockSpec(memory_space=pltpu.VMEM)

OUTER = (0, 1, 6, 7)
INNER = (2, 3, 4, 5)
TO_INNER = [(i, i ^ 2) for i in OUTER]
ACROSS = [(i, i ^ 6) for i in INNER]
TO_OUTER = [(i, i ^ 2) for i in INNER]
TO_DIAG = [(i, i ^ 3) for i in INNER]
OVER_Y = [(i, i ^ 1) for i in range(8)]
OVER_Y_INNER = [(i, i ^ 1) for i in INNER]

OWN = 4
COUNTS = (12, 13, 14, 16)

LIST, STRAIGHT, DIAG, SIDE, SLOTS, BRANCH, CODES = 0, 16, 20, 24, 32, 48, 64


def is_inner(me):
    return ((me >> 1) ^ (me >> 2)) & 1


def bits(mask):
    total = mask & 1
    for i in range(1, 8):
        total = total + ((mask >> i) & 1)
    return total


def cost(nbytes, flops=0):
    return pl.CostEstimate(flops=flops, bytes_accessed=nbytes, transcendentals=0)


def start_kernel(me_ref, doc_ref, sample_ref, grad_ref, tab_ref, place_ref, across_ref, straight_ref,
                 diag_ref, side_ref, next_ref, seen, own, sems, *, off):
    me = me_ref[0]
    owners = 8
    for d in range(owners):
        seen[d] = 0
    for i in range(owners * CAP):
        tab_ref[i] = 0
    mask = jnp.int32(0)
    half = me >> 2
    for p in range(owners * CAP):
        doc = doc_ref[p, 0]
        slot = doc * CAP + jnp.minimum(seen[doc], CAP - 1)
        seen[doc] = seen[doc] + 1
        place_ref[p] = slot
        tab_ref[slot] = sample_ref[p]
        bit = jnp.left_shift(1, sample_ref[p])
        mask = jnp.where((doc >> 2) != half, mask | bit, mask)
    for k in range(8):
        own[k] = 0
    count = jnp.int32(0)
    for s in range(8):
        hit = (mask >> s) & 1
        own[jnp.where(hit == 1, count, 8)] = s
        count = count + hit
    width = next_ref.shape[2]
    copies = []

    def go(src, dst):
        c = pltpu.make_async_copy(src, dst, sems.at[len(copies)])
        c.start()
        copies.append(c)

    for k in range(OWN):
        go(grad_ref.at[own[k]], across_ref.at[k])
    for r in range(CAP):
        go(grad_ref.at[tab_ref[(me ^ 2) * CAP + r]], straight_ref.at[r])
        go(grad_ref.at[tab_ref[(me ^ 3) * CAP + r]], diag_ref.at[r])
        go(grad_ref.at[tab_ref[(me ^ 1) * CAP + r]], side_ref.at[r])
    for s in range(8):
        go(grad_ref.at[s, :, pl.ds(off, width)], next_ref.at[s])
    for c in copies:
        c.wait()


def start_call(me, pair_doc, pair_sample, grad, off):
    n, rows, width = grad.shape
    def buf(k, w):
        return jax.ShapeDtypeStruct((k, rows, w), grad.dtype)
    table = jax.ShapeDtypeStruct((8 * CAP,), jnp.int32)
    return pl.pallas_call(
        functools.partial(start_kernel, off=off),
        out_shape=(table, table, buf(OWN, width), buf(CAP, width), buf(CAP, width), buf(CAP, width),
                   buf(n, width - off)),
        in_specs=[SMEM, SMEM, SMEM, ANY],
        out_specs=(SMEM, SMEM, ANY, ANY, ANY, ANY, ANY),
        scratch_shapes=[pltpu.SMEM((8,), jnp.int32), pltpu.SMEM((16,), jnp.int32),
                        pltpu.SemaphoreType.DMA((OWN + 3 * CAP + n,))],
        cost_estimate=cost(6_000_000),
    )(me, pair_doc, pair_sample, grad)


def own_kernel(me_ref, tab_ref, act_ref, token_ref, straight_ref, diag_ref, side_ref, sems):
    me = me_ref[0]
    copies = []
    for r in range(CAP):
        for turn, dst in ((2, straight_ref), (3, diag_ref), (1, side_ref)):
            c = pltpu.make_async_copy(
                act_ref.at[tab_ref[(me ^ turn) * CAP + r]], dst.at[r], sems.at[len(copies)]
            )
            c.start()
            copies.append(c)
    for c in copies:
        c.wait()


def own_call(me, tab, act, token):
    buf = jax.ShapeDtypeStruct((CAP,) + act.shape[1:], act.dtype)
    return pl.pallas_call(
        own_kernel,
        out_shape=(buf,) * 3,
        in_specs=[SMEM, SMEM, ANY, ANY],
        out_specs=(ANY,) * 3,
        scratch_shapes=[pltpu.SemaphoreType.DMA((3 * CAP,))],
        cost_estimate=cost(4_000_000),
    )(me, tab, act, token)


def codes_kernel(me_ref, all_ref, out_ref, scratch, masks, *, groups):
    group, me = me_ref[1], me_ref[0]
    base = group * 8

    def owner_mask(row, _):
        first = jnp.where((row & 7) < 4, 8, 0)
        mask = jnp.int32(0)
        for j in range(8):
            mask = mask | jnp.left_shift(1, all_ref[row, first + j])
        masks[row] = mask
        return 0

    lax.fori_loop(0, groups * 8, owner_mask, 0)

    def longest(k, best):
        row = (k >> 2) * 8 + 2 + (k & 3)
        return jnp.maximum(best, jnp.maximum(bits(masks[row]), OWN) + bits(masks[row ^ 2]))

    best = lax.fori_loop(0, groups * 4, longest, jnp.int32(0))
    branch = jnp.int32(0)
    for c in COUNTS[:-1]:
        branch = branch + (best > c).astype(jnp.int32)
    for i in range(CODES):
        out_ref[i] = 0
    for i in range(32):
        scratch[i] = 0
    out_ref[BRANCH] = branch
    inner = is_inner(me)
    mine, partner = masks[base + me], masks[base + (me ^ 2)]
    count = jnp.int32(0)
    for s in range(8):
        hit = (mine >> s) & 1
        scratch[jnp.where(hit == 1, count, 31)] = s
        count = count + hit
    count = jnp.maximum(count, OWN)
    for s in range(8):
        hit = (partner >> s) & 1
        scratch[jnp.where(hit == 1, count, 31)] = 8 + s
        count = count + hit
    for k in range(16):
        out_ref[LIST + k] = scratch[k]
    far, far_outer = masks[base + (me ^ 6)], masks[base + (me ^ 4)]
    after = jnp.maximum(bits(far), OWN)

    def place(near, doc, r):
        owner = base + ((me ^ 6) if near else (me ^ 4))
        sample = all_ref[owner, doc * CAP + r]
        below = jnp.left_shift(1, sample) - 1
        return (bits(far & below) if near else after + bits(far_outer & below)) * inner

    for r in range(CAP):
        out_ref[STRAIGHT + r] = place(True, me ^ 2, r)
        out_ref[STRAIGHT + CAP + r] = place(False, me ^ 2, r)
        out_ref[DIAG + r] = place(True, me ^ 3, r)
        out_ref[DIAG + CAP + r] = place(False, me ^ 3, r)
        out_ref[SIDE + r] = all_ref[base + (me ^ 2), (me ^ 1) * CAP + r]
        out_ref[SIDE + CAP + r] = place(True, me ^ 1, r)
        out_ref[SIDE + 2 * CAP + r] = place(False, me ^ 1, r)
        out_ref[SLOTS + r] = all_ref[base + me, me * CAP + r]
        out_ref[SLOTS + CAP + r] = all_ref[base + (me ^ 2), me * CAP + r]
        out_ref[SLOTS + 2 * CAP + r] = place(True, me, r)
        out_ref[SLOTS + 3 * CAP + r] = place(False, me, r)


def codes_call(me, tables, groups):
    return pl.pallas_call(
        functools.partial(codes_kernel, groups=groups),
        out_shape=jax.ShapeDtypeStruct((CODES,), jnp.int32),
        in_specs=[SMEM, SMEM],
        out_specs=SMEM,
        scratch_shapes=[pltpu.SMEM((32,), jnp.int32), pltpu.SMEM((groups * 8,), jnp.int32)],
        cost_estimate=cost(4096),
    )(me, tables)


def mix_kernel(codes_ref, own_ref, came_ref, *rest, first, off, ahead):
    if ahead is None:
        token_ref, list_ref, sems = rest
    else:
        token_ref, ahead_ref, list_ref, next_ref, sems = rest
    count, _, width = list_ref.shape
    for k in range(count):
        code = codes_ref[LIST + first + k]

        @pl.when(code < 8)
        def _():
            pltpu.make_async_copy(
                own_ref.at[code, :, pl.ds(off, width)], list_ref.at[k], sems.at[k]
            ).start()

        @pl.when(code >= 8)
        def _():
            pltpu.make_async_copy(came_ref.at[code - 8], list_ref.at[k], sems.at[k]).start()

    copies = []
    if ahead is not None:
        for s in range(8):
            c = pltpu.make_async_copy(
                ahead_ref.at[s, :, pl.ds(ahead, next_ref.shape[2])], next_ref.at[s], sems.at[count + s]
            )
            c.start()
            copies.append(c)
    for k in range(count):
        pltpu.make_async_copy(came_ref.at[0], list_ref.at[k], sems.at[k]).wait()
    for c in copies:
        c.wait()


def mix_call(codes, own, came, count, first, off, token, ahead_array, ahead, ahead_width):
    n, rows, width = came.shape
    out = [jax.ShapeDtypeStruct((count, rows, width), own.dtype)]
    args = [codes, own, came, token]
    if ahead is not None:
        out.append(jax.ShapeDtypeStruct((n, rows, ahead_width), own.dtype))
        args.append(ahead_array)
    return pl.pallas_call(
        functools.partial(mix_kernel, first=first, off=off, ahead=ahead),
        out_shape=tuple(out),
        in_specs=[SMEM] + [ANY] * (len(args) - 1),
        out_specs=(ANY,) * len(out),
        scratch_shapes=[pltpu.SemaphoreType.DMA((count + n,))],
        cost_estimate=cost(4_000_000),
    )(*args)


def fetch(code, early_ref, late_ref, off, dst, sem):
    width = dst.shape[1]
    if early_ref is None:
        pltpu.make_async_copy(late_ref.at[code], dst, sem).start()
        return

    @pl.when(code < OWN)
    def _():
        pltpu.make_async_copy(early_ref.at[code, :, pl.ds(off, width)], dst, sem).start()

    @pl.when(code >= OWN)
    def _():
        pltpu.make_async_copy(late_ref.at[code - OWN], dst, sem).start()


def forward_kernel(codes_ref, came_ref, *rest, split, off):
    if split:
        early_ref, late_ref, token_ref, straight_ref, diag_ref, side_ref, sems = rest
    else:
        late_ref, token_ref, straight_ref, diag_ref, side_ref, sems = rest
        early_ref = None
    waits = []
    for k in range(2 * CAP):
        for at, dst in ((STRAIGHT, straight_ref), (DIAG, diag_ref)):
            fetch(codes_ref[at + k], early_ref, late_ref, off, dst.at[k], sems.at[len(waits)])
            waits.append(dst.at[k])
    for k in range(CAP):
        pltpu.make_async_copy(came_ref.at[codes_ref[SIDE + k]], side_ref.at[k], sems.at[len(waits)]).start()
        waits.append(side_ref.at[k])
    for k in range(CAP, 3 * CAP):
        fetch(codes_ref[SIDE + k], early_ref, late_ref, off, side_ref.at[k], sems.at[len(waits)])
        waits.append(side_ref.at[k])
    for i, dst in enumerate(waits):
        pltpu.make_async_copy(came_ref.at[0], dst, sems.at[i]).wait()


def forward_call(codes, came, early, late, off, token):
    n, rows, width = came.shape

    def buf(k):
        return jax.ShapeDtypeStruct((k, rows, width), came.dtype)

    args = [codes, came] + ([] if early is None else [early]) + [late, token]
    return pl.pallas_call(
        functools.partial(forward_kernel, split=early is not None, off=off),
        out_shape=(buf(2 * CAP), buf(2 * CAP), buf(3 * CAP)),
        in_specs=[SMEM] + [ANY] * (len(args) - 1),
        out_specs=(ANY,) * 3,
        scratch_shapes=[pltpu.SemaphoreType.DMA((7 * CAP,))],
        cost_estimate=cost(4_000_000),
    )(*args)


def gram_kernel(me_ref, codes_ref, own_ref, came_ref, *rest, split, off, mode, last):
    rest = list(rest)
    early_ref = rest.pop(0) if split else None
    (late_ref, own_straight_ref, own_diag_ref, own_side_ref, straight_ref, diag_ref, side_ref, doc_ref,
     token_ref) = rest[:9]
    rest = rest[9:]
    held = [rest.pop(0) for _ in range({"first": 0, "next": 1, "score": 2}[mode])]
    out_ref, rows_ref, cols_ref, acc_ref, sems = rest
    me = me_ref[0]
    inner = is_inner(me)
    rows = own_ref.shape[1]
    width = rows_ref.shape[1]
    docs = pltpu.make_async_copy(doc_ref.at[0, :, pl.ds(off, width)], cols_ref, sems.at[8 * CAP])
    docs.start()

    def slot(k):
        return rows_ref.at[pl.ds(k * rows, rows), :]

    def wide(ref, i):
        return ref.at[i, :, pl.ds(off, width)]

    def go(src, k):
        pltpu.make_async_copy(src, slot(k), sems.at[k]).start()

    for r in range(CAP):
        go(wide(own_ref, codes_ref[SLOTS + r]), r)
        go(wide(own_side_ref, r), 4 * CAP + r)

    @pl.when(inner == 1)
    def _():
        for r in range(CAP):
            go(came_ref.at[codes_ref[SLOTS + CAP + r]], CAP + r)
        for k in range(2 * CAP, 4 * CAP):
            fetch(codes_ref[SLOTS + k], early_ref, late_ref, off, slot(k), sems.at[k])
        for k in range(3 * CAP):
            go(side_ref.at[k], 5 * CAP + k)

    @pl.when(inner == 0)
    def _():
        for r in range(CAP):
            go(wide(own_straight_ref, r), CAP + r)
            go(wide(own_diag_ref, r), 5 * CAP + r)
        for k in range(2 * CAP):
            go(straight_ref.at[k], 2 * CAP + k)
            go(diag_ref.at[k], 6 * CAP + k)

    for k in range(8 * CAP):
        pltpu.make_async_copy(came_ref.at[0], slot(k), sems.at[k]).wait()
    docs.wait()
    step = 256
    if mode == "score":
        acc_ref[...] = held[1][...]

    def block(n, _):
        at = pl.ds(pl.multiple_of(n * step, step), step)
        part = lax.dot_general(
            rows_ref[...], cols_ref[at, :], (((1,), (1,)), ((), ())), preferred_element_type=jnp.float32
        )
        if mode == "first":
            out_ref[:, at] = part
        elif mode == "next":
            out_ref[:, at] = held[0][:, at] + part
        else:
            both = part * held[0][:, at]
            acc_ref[...] += jnp.sum(both.reshape(8 * CAP, rows, step), axis=1)
        return 0

    lax.fori_loop(0, SEQ_D // step, block, 0)
    if mode == "score" and not last:
        out_ref[...] = acc_ref[...]
    if last:
        total = jnp.sum(acc_ref[...], axis=1, keepdims=True)
        out_ref[...] = jnp.zeros_like(out_ref)
        near = jnp.where(inner == 1, me ^ 6, me ^ 4)
        far = jnp.where(inner == 1, me ^ 4, me ^ 6)
        for k, owner in enumerate((me, me ^ 2, near, far, me ^ 1, me ^ 3, near ^ 1, far ^ 1)):
            wide_total = jnp.broadcast_to(total[k * CAP : (k + 1) * CAP], (CAP, 128))
            out_ref[owner] = wide_total


def gram_call(me, codes, own, came, early, late, owns, parts, doc, off, token, mode, held, last=False):
    n, rows, width = came.shape
    tokens = doc.shape[1]
    total = 8 * CAP * rows
    args = [me, codes, own, came] + ([] if early is None else [early]) + [late, *owns, *parts, doc, token]
    if last:
        out = jax.ShapeDtypeStruct((8, CAP, 128), jnp.float32)
    elif mode == "score":
        out = jax.ShapeDtypeStruct((8 * CAP, 256), jnp.float32)
    else:
        out = jax.ShapeDtypeStruct((total, tokens), jnp.float32)
    return pl.pallas_call(
        functools.partial(gram_kernel, split=early is not None, off=off, mode=mode, last=last),
        out_shape=out,
        in_specs=[SMEM, SMEM] + [ANY] * (len(args) - 2) + [VMEM] * len(held),
        out_specs=VMEM,
        scratch_shapes=[
            pltpu.VMEM((total, width), doc.dtype),
            pltpu.VMEM((tokens, width), doc.dtype),
            pltpu.VMEM((8 * CAP, 256), jnp.float32),
            pltpu.SemaphoreType.DMA((8 * CAP + 1,)),
        ],
        compiler_params=pltpu.CompilerParams(vmem_limit_bytes=24 * 1024 * 1024),
        cost_estimate=cost(4_000_000, 2 * total * tokens * width),
    )(*args, *held)


def finish_kernel(came_ref, place_ref, out_ref, *, tensor):
    factor = 1.0 / jnp.sqrt(jnp.float32(FF) * jnp.float32(D) * jnp.float32(SEQ_S) * jnp.float32(SEQ_D))
    for p in range(8 * CAP):
        slot = place_ref[p]
        doc, r = slot // CAP, slot % CAP
        total = came_ref[doc * tensor, r]
        for t in range(1, tensor):
            total = total + came_ref[doc * tensor + t, r]
        out_ref[p] = total * factor


def pieces(width, parts):
    lanes = width // 128
    sizes = [(lanes // parts + (1 if i < lanes % parts else 0)) * 128 for i in range(parts)]
    sizes[-1] += width - sum(sizes)
    return sizes


def chain(sample_act, sample_grad, doc_act, doc_grad, pair_doc, pair_sample):
    groups, tensor = lax.axis_size("groups"), lax.axis_size("tensor")
    me = jnp.stack([lax.axis_index("docs"), lax.axis_index("groups")]).astype(jnp.int32)
    chunks = []
    off = 0
    for w in pieces(sample_grad.shape[2], 2):
        chunks.append((True, off, w))
        off += w
    off = 0
    for w in pieces(sample_act.shape[2], 6):
        chunks.append((False, off, w))
        off += w
    send = lambda x, pairs: lax.ppermute(x, "docs", pairs)
    came0 = send(sample_grad[:, :, : chunks[0][2]], TO_INNER)
    tab, place, across, straight, diag, side, out1 = start_call(
        me, pair_doc, pair_sample, sample_grad, chunks[1][1]
    )
    early = send(across, ACROSS)
    own_grads = (send(straight, TO_OUTER), send(diag, TO_DIAG), send(side, OVER_Y))
    tables = lax.all_to_all(
        jnp.broadcast_to(tab[None, :], (groups * 8, 8 * CAP)), ("groups", "docs"), 0, 0, tiled=True
    )
    codes = codes_call(me, tables, groups)

    def pipeline(count, came0, early, own_grads, out1, codes, sample_act, sample_grad, doc_act, doc_grad):
        total = len(chunks)
        sample = lambda i: sample_grad if chunks[i][0] else sample_act
        came = {0: came0, 1: send(out1, TO_INNER)}
        late, parts, token = {}, {}, codes
        state = dict(grads=None, score=None, owns=None)

        def mix(i, token):
            is_grad, off, w = chunks[i]
            ahead = i + 2 if i + 2 < total else None
            first = OWN if is_grad else 0
            out = mix_call(
                codes, sample(i), came[i], count - first, first, off, token,
                None if ahead is None else sample(ahead),
                None if ahead is None else chunks[ahead][1],
                None if ahead is None else chunks[ahead][2],
            )
            late[i] = send(out[0], ACROSS)
            if ahead is not None:
                came[ahead] = send(out[1], TO_INNER)
            return out[0]

        def forward(i, token):
            is_grad, off, w = chunks[i]
            s, d, y = forward_call(codes, came[i], early if is_grad else None, late[i], off, token)
            parts[i] = (send(s, TO_OUTER), send(d, TO_DIAG), send(y, OVER_Y_INNER))
            return s

        def gram(i, token):
            is_grad, off, w = chunks[i]
            if is_grad:
                held = [] if state["grads"] is None else [state["grads"]]
                mode = "next" if held else "first"
                out = gram_call(me, codes, sample_grad, came[i], early, late[i], own_grads, parts[i],
                                doc_grad, off, token, mode, held)
                state["grads"] = out
                if not chunks[i + 1][0]:
                    state["grads"] = lax.psum(out, "tensor") if tensor != 2 else out + lax.ppermute(
                        out, "tensor", [(0, 1), (1, 0)]
                    )
                    state["score"] = jnp.zeros((8 * CAP, 256), jnp.float32)
                return out
            out = gram_call(me, codes, sample_act, came[i], None, late[i], state["owns"], parts[i],
                            doc_act, off, token, "score", [state["grads"], state["score"]],
                            last=i == total - 1)
            state["score"] = out
            return out

        token = mix(0, token)
        s, d, y = own_call(me, tab, sample_act, token)
        state["owns"] = (send(s, TO_OUTER), send(d, TO_DIAG), send(y, OVER_Y))
        token = mix(1, s)
        for i in range(total):
            if i + 2 < total:
                token = mix(i + 2, token)
            token = forward(i, token)
            if i >= 2:
                token = gram(i - 2, token)
        for i in range(total - 2, total):
            token = gram(i, token)
        return state["score"]

    score = lax.switch(
        codes[BRANCH],
        [functools.partial(pipeline, c) for c in COUNTS],
        came0, early, own_grads, out1, codes, sample_act, sample_grad, doc_act, doc_grad,
    )
    give = jnp.broadcast_to(score[:, None, :, 0], (8, tensor, CAP)).reshape(8 * tensor, CAP)
    back = lax.all_to_all(give, ("docs", "tensor"), 0, 0, tiled=True)
    return pl.pallas_call(
        functools.partial(finish_kernel, tensor=tensor),
        out_shape=jax.ShapeDtypeStruct((8 * CAP,), jnp.float32),
        in_specs=[SMEM, SMEM],
        out_specs=SMEM,
    )(back, place)


def direct(sample_act, sample_grad, doc_act, doc_grad, pair_doc, pair_sample):
    owners = lax.axis_size("docs")
    pair_count = pair_doc.shape[0]
    slot_count = owners * CAP
    factor = 1.0 / jnp.sqrt(
        jnp.float32(FF) * jnp.float32(D) * jnp.float32(SEQ_S) * jnp.float32(SEQ_D)
    )
    target = pair_doc[:, 0]
    order = jnp.arange(pair_count, dtype=jnp.int32)
    earlier = (target[:, None] == target[None, :]) & (order[None, :] < order[:, None])
    rank = jnp.sum(earlier.astype(jnp.int32), axis=1)
    slot_of_pair = target * CAP + rank
    chosen = (jnp.arange(slot_count, dtype=jnp.int32)[:, None] == slot_of_pair[None, :]).astype(
        jnp.int32
    )
    slot_sample = jnp.sum(chosen * pair_sample[None, :], axis=1)
    send_act = sample_act[slot_sample]
    send_grad = sample_grad[slot_sample]
    send_act = send_act.reshape(owners, CAP, send_act.shape[1], send_act.shape[2])
    send_grad = send_grad.reshape(owners, CAP, send_grad.shape[1], send_grad.shape[2])
    grad_in = lax.all_to_all(send_grad, "docs", split_axis=0, concat_axis=0, tiled=True)
    act_in = lax.all_to_all(send_act, "docs", split_axis=0, concat_axis=0, tiled=True)
    grad_gram = jnp.einsum("nmsf,tf->nmst", grad_in, doc_grad[0], preferred_element_type=jnp.float32)
    grad_sum = lax.psum(grad_gram, "tensor")
    act_gram = jnp.einsum("nmsf,tf->nmst", act_in, doc_act[0], preferred_element_type=jnp.float32)
    scores = lax.psum(jnp.sum(act_gram * grad_sum, axis=(2, 3)) * factor, "tensor")
    returned = lax.all_to_all(scores, "docs", split_axis=0, concat_axis=0, tiled=True)
    flat_scores = returned.reshape(slot_count)
    return jnp.sum(jnp.where(chosen > 0, flat_scores[:, None], 0.0), axis=0)


def solution(mesh):
    in_specs = (
        P(("groups", "docs"), None, "tensor"),
        P(("groups", "docs"), None, "tensor"),
        P(("groups", "docs"), None, "tensor"),
        P(("groups", "docs"), None, "tensor"),
        P(("groups", "docs"), None),
        P(("groups", "docs")),
    )
    out_specs = P(("groups", "docs"))

    def per_device(sample_act, sample_grad, doc_act, doc_grad, pair_doc, pair_sample):
        fits = mesh.shape["docs"] == 8 and pair_doc.shape[0] == 8 * CAP and sample_act.shape[0] == 8
        run = chain if fits else direct
        return run(sample_act, sample_grad, doc_act, doc_grad, pair_doc, pair_sample)

    return jax.shard_map(
        per_device, mesh=mesh, in_specs=in_specs, out_specs=out_specs, check_vma=False
    )
```

```python
import functools

import jax
import jax.numpy as jnp
from jax import lax
from jax.experimental import pallas as pl
from jax.experimental.pallas import tpu as pltpu
from jax.sharding import PartitionSpec as P

FF = 11008
D = 4096
SEQ_S = 32
SEQ_D = 768
CAP = 2

ANY = pl.BlockSpec(memory_space=pl.ANY)
SMEM = pl.BlockSpec(memory_space=pltpu.SMEM)
VMEM = pl.BlockSpec(memory_space=pltpu.VMEM)

INNER = (2, 3, 4, 5)
ACROSS = [(i, i ^ 6) for i in INNER]
OVER_Z = [(i, i ^ 2) for i in range(8)]
OVER_Y = [(i, i ^ 1) for i in range(8)]

OWN = 4
MAIN = 12
EXTRAS = (0, 1, 2, 4)

LIST, STRAIGHT, DIAG, SIDE, SLOTS, BRANCH, CODES = 0, 16, 20, 24, 32, 48, 64
SENT = 16


def is_inner(me):
    return ((me >> 1) ^ (me >> 2)) & 1


def bits(mask):
    total = mask & 1
    for i in range(1, 8):
        total = total + ((mask >> i) & 1)
    return total


SMALL = pltpu.CompilerParams(vmem_limit_bytes=6 * 1024 * 1024)
CHEAP = pl.CostEstimate(flops=0, bytes_accessed=1024, transcendentals=0)
CHUNK = 1024
LEAD = 4


class Copies:
    def __init__(self, sems):
        self.sems, self.used, self.held = sems, 0, []

    def start(self, src, dst):
        copy = pltpu.make_async_copy(src, dst, self.sems.at[self.used])
        copy.start()
        self.used += 1
        self.held.append(copy)

    def either(self, first, src, other, dst):
        sem = self.sems.at[self.used]

        @pl.when(first)
        def _():
            pltpu.make_async_copy(src, dst, sem).start()

        @pl.when(jnp.logical_not(first))
        def _():
            pltpu.make_async_copy(other, dst, sem).start()

        self.used += 1
        self.held.append(pltpu.make_async_copy(src, dst, sem))

    def wait(self):
        for copy in self.held:
            copy.wait()
        self.held = []


def cut(ref, i, off, width):
    return ref.at[i, :, pl.ds(off, width)]


def own_slots(copies, inner, me, tab_ref, here, ahead, dst):
    @pl.when(inner == 1)
    def _():
        c = Copies(copies.sems)
        for part, (ref, off, width) in enumerate(here):
            for k in range(2 * CAP):
                sample = tab_ref[(me ^ (2 + k // CAP)) * CAP + k % CAP]
                c.start(cut(ref, sample, off, width), cut(dst, part * 2 * CAP + k, 0, width))
        c.wait()

    @pl.when(inner == 0)
    def _():
        c = Copies(copies.sems)
        ref, off, width = ahead
        for s in range(8):
            c.start(cut(ref, s, off, width), cut(dst, s, 0, width))
        c.wait()


def start_kernel(me_ref, doc_ref, sample_ref, grad_ref, act_ref, tab_ref, place_ref, own_ref, z_ref, across_ref,
                 seen, sems, out_sems):
    me = me_ref[0]
    inner = is_inner(me)
    for d in range(8):
        seen[d] = 0
    for i in range(8 * CAP):
        tab_ref[i] = 0
    for i in range(16):
        own_ref[i] = 0
    mask = jnp.int32(0)
    half = me >> 2
    for p in range(8 * CAP):
        doc = doc_ref[p, 0]
        slot = doc * CAP + jnp.minimum(seen[doc], CAP - 1)
        seen[doc] = seen[doc] + 1
        place_ref[p] = slot
        tab_ref[slot] = sample_ref[p]
        bit = jnp.left_shift(1, sample_ref[p])
        mask = jnp.where((doc >> 2) != half, mask | bit, mask)
    count = jnp.int32(0)
    for s in range(8):
        hit = (mask >> s) & 1
        own_ref[jnp.where(hit == 1, count, 8)] = s
        count = count + hit
    width = grad_ref.shape[2] // 2
    lists = Copies(sems)
    for k in range(OWN):
        lists.start(cut(grad_ref, own_ref[k], 0, 2 * width), across_ref.at[k])
    own_slots(Copies(out_sems), inner, me, tab_ref,
              ((grad_ref, 0, width), (grad_ref, width, width)), (grad_ref, 0, width), z_ref)
    lists.wait()


def start_call(me, pair_doc, pair_sample, grad, act):
    rows, width = grad.shape[1:]
    table = jax.ShapeDtypeStruct((16,), jnp.int32)
    return pl.pallas_call(
        start_kernel,
        out_shape=(table, table, table, jax.ShapeDtypeStruct((8, rows, CHUNK), grad.dtype),
                   jax.ShapeDtypeStruct((OWN, rows, width), grad.dtype)),
        in_specs=[SMEM, SMEM, SMEM, ANY, ANY],
        out_specs=(SMEM, SMEM, SMEM, VMEM, VMEM),
        scratch_shapes=[pltpu.SMEM((8,), jnp.int32), pltpu.SemaphoreType.DMA((OWN,)),
                        pltpu.SemaphoreType.DMA((8,))],
        compiler_params=SMALL,
        cost_estimate=CHEAP,
    )(me, pair_doc, pair_sample, grad, act)


def second_kernel(me_ref, tab_ref, own_ref, grad_ref, act_ref, token_ref, z_ref, across_ref, sems, out_sems):
    me = me_ref[0]
    inner = is_inner(me)
    lists = Copies(sems)
    for k in range(OWN):
        lists.start(cut(act_ref, own_ref[k], 0, 2 * CHUNK), across_ref.at[k])
    own_slots(Copies(out_sems), inner, me, tab_ref,
              ((act_ref, 0, CHUNK), (act_ref, CHUNK, CHUNK)), (grad_ref, CHUNK, CHUNK), z_ref)
    lists.wait()


def second_call(me, tab, own, grad, act, token):
    rows = grad.shape[1]

    def buf(k, w):
        return jax.ShapeDtypeStruct((k, rows, w), grad.dtype)

    return pl.pallas_call(
        second_kernel,
        out_shape=(buf(8, CHUNK), buf(OWN, 2 * CHUNK)),
        in_specs=[SMEM, SMEM, SMEM, ANY, ANY, ANY],
        out_specs=(VMEM,) * 2,
        scratch_shapes=[pltpu.SemaphoreType.DMA((OWN,)), pltpu.SemaphoreType.DMA((8,))],
        compiler_params=SMALL,
        cost_estimate=CHEAP,
    )(me, tab, own, grad, act, token)


def third_kernel(me_ref, tab_ref, act_ref, token_ref, z2_ref, z3_ref, out_sems, *, rest):
    me = me_ref[0]
    inner = is_inner(me)
    own_slots(Copies(out_sems), inner, me, tab_ref,
              ((act_ref, 2 * CHUNK, CHUNK), (act_ref, 3 * CHUNK, CHUNK)), (act_ref, 0, CHUNK), z2_ref)
    own_slots(Copies(out_sems), inner, me, tab_ref,
              ((act_ref, 4 * CHUNK, CHUNK), (act_ref, 5 * CHUNK, rest)), (act_ref, CHUNK, CHUNK), z3_ref)


def third_call(me, tab, act, token):
    rows, width = act.shape[1:]
    buf = jax.ShapeDtypeStruct((8, rows, CHUNK), act.dtype)
    return pl.pallas_call(
        functools.partial(third_kernel, rest=width - 5 * CHUNK),
        out_shape=(buf, buf),
        in_specs=[SMEM, SMEM, ANY, ANY],
        out_specs=(VMEM,) * 2,
        scratch_shapes=[pltpu.SemaphoreType.DMA((8,))],
        compiler_params=SMALL,
        cost_estimate=CHEAP,
    )(me, tab, act, token)


def mix_kernel(me_ref, codes_ref, own_ref, came_ref, token_ref, list_ref, sems, *, first, off):
    count, _, width = list_ref.shape

    @pl.when(is_inner(me_ref[0]) == 1)
    def _():
        copies = Copies(sems)
        for k in range(count):
            code = codes_ref[LIST + first + k]
            mine = code < 8
            copies.either(mine, cut(own_ref, jnp.minimum(code, 7), off, width),
                          cut(came_ref, jnp.maximum(code - 8, 0), 0, width), list_ref.at[k])
        copies.wait()


def mix_call(me, codes, own, came, count, first, off, width, token):
    rows = own.shape[1]
    return pl.pallas_call(
        functools.partial(mix_kernel, first=first, off=off),
        out_shape=jax.ShapeDtypeStruct((count, rows, width), own.dtype),
        in_specs=[SMEM, SMEM, ANY, ANY, ANY],
        out_specs=VMEM,
        scratch_shapes=[pltpu.SemaphoreType.DMA((count,))],
        compiler_params=SMALL,
        cost_estimate=CHEAP,
    )(me, codes, own, came, token)


def entry(copies, code, came_over, width, dst):
    early, late_ref, (extra_ref, extra_off) = came_over
    sem = copies.sems.at[copies.used]
    copies.used += 1
    skip = 0 if early is None else OWN

    @pl.when(code >= SENT)
    def _():
        pltpu.make_async_copy(cut(extra_ref, jnp.maximum(code - SENT, 0), extra_off, width), dst, sem).start()

    @pl.when((code >= skip) & (code < SENT))
    def _():
        at = jnp.clip(code - skip, 0, late_ref.shape[0] - 1)
        pltpu.make_async_copy(cut(late_ref, at, 0, width), dst, sem).start()

    if early is not None:
        @pl.when(code < OWN)
        def _():
            pltpu.make_async_copy(cut(early[0], jnp.minimum(code, OWN - 1), early[1], width), dst, sem).start()

    copies.held.append(pltpu.make_async_copy(cut(late_ref, 0, 0, width), dst, sem))


def over(rest, early_off, extra_off):
    early = None if early_off is None else (rest.pop(0), early_off)
    return early, rest.pop(0), (rest.pop(0), extra_off)


def ahead_kernel(own_ref, grad_ref, act_ref, grad_out, act_out, sems):
    copies = Copies(sems)
    for k in range(grad_out.shape[0]):
        copies.start(grad_ref.at[own_ref[OWN + k]], grad_out.at[k])
        copies.start(act_ref.at[own_ref[OWN + k]], act_out.at[k])
    copies.wait()


def ahead_call(count, own, grad, act):
    return pl.pallas_call(
        ahead_kernel,
        out_shape=tuple(jax.ShapeDtypeStruct((count,) + x.shape[1:], x.dtype) for x in (grad, act)),
        in_specs=[SMEM, ANY, ANY],
        out_specs=(VMEM, VMEM),
        scratch_shapes=[pltpu.SemaphoreType.DMA((2 * count,))],
        compiler_params=SMALL,
        cost_estimate=CHEAP,
    )(own, grad, act)


def forward_kernel(me_ref, codes_ref, *rest, offs, ahead):
    rest = list(rest)
    came_over = over(rest, *offs)
    ahead_ref, token_ref, z_ref, sems = rest
    inner = is_inner(me_ref[0])
    width = came_over[1].shape[2]

    @pl.when(inner == 1)
    def _():
        copies = Copies(sems)
        for k in range(2 * CAP):
            entry(copies, codes_ref[STRAIGHT + k], came_over, width, cut(z_ref, k, 0, width))
            entry(copies, codes_ref[DIAG + k], came_over, width, cut(z_ref, 2 * CAP + k, 0, width))
        copies.wait()

    if ahead is not None:
        @pl.when(inner == 0)
        def _():
            copies = Copies(sems)
            off, some = ahead
            for s in range(8):
                copies.start(cut(ahead_ref, s, off, some), cut(z_ref, s, 0, some))
            copies.wait()


def forward_call(me, codes, arrays, offs, ahead_array, ahead, token):
    late = arrays[-2]
    rows, width = late.shape[1:]
    args = [me, codes, *arrays, ahead_array, token]
    return pl.pallas_call(
        functools.partial(forward_kernel, offs=offs, ahead=ahead),
        out_shape=jax.ShapeDtypeStruct((8, rows, width), late.dtype),
        in_specs=[SMEM, SMEM] + [ANY] * (len(args) - 2),
        out_specs=VMEM,
        scratch_shapes=[pltpu.SemaphoreType.DMA((8,))],
        compiler_params=SMALL,
        cost_estimate=CHEAP,
    )(*args)


def side_kernel(me_ref, codes_ref, tab_ref, sample_ref, came_ref, *rest, offs, off, part):
    rest = list(rest)
    came_over = over(rest, *offs)
    own_ref, far_ref, token_ref, side_ref, sems, role_sems = rest
    me = me_ref[0]
    inner = is_inner(me)
    width = side_ref.shape[2]
    mine = Copies(sems)
    for r in range(CAP):
        mine.start(cut(sample_ref, tab_ref[(me ^ 1) * CAP + r], off, width), side_ref.at[r])

    @pl.when(inner == 1)
    def _():
        copies = Copies(role_sems)
        for k in range(CAP):
            copies.start(cut(came_ref, codes_ref[SIDE + k], 0, width), side_ref.at[CAP + k])
        for k in range(CAP, 3 * CAP):
            entry(copies, codes_ref[SIDE + k], came_over, width, side_ref.at[CAP + k])
        copies.wait()

    @pl.when(inner == 0)
    def _():
        copies = Copies(role_sems)
        for k in range(CAP):
            copies.start(cut(own_ref, part * 2 * CAP + CAP + k, 0, width), side_ref.at[CAP + k])
        for k in range(2 * CAP):
            copies.start(cut(far_ref, 2 * CAP + k, 0, width), side_ref.at[2 * CAP + k])
        copies.wait()

    mine.wait()


def side_call(me, codes, tab, sample, came, arrays, offs, own, far, off, part, token):
    late = arrays[-2]
    rows, width = late.shape[1:]
    args = [me, codes, tab, sample, came, *arrays, own, far, token]
    return pl.pallas_call(
        functools.partial(side_kernel, offs=offs, off=off, part=part),
        out_shape=jax.ShapeDtypeStruct((4 * CAP, rows, width), late.dtype),
        in_specs=[SMEM, SMEM, SMEM] + [ANY] * (len(args) - 3),
        out_specs=VMEM,
        scratch_shapes=[pltpu.SemaphoreType.DMA((CAP,)), pltpu.SemaphoreType.DMA((3 * CAP,))],
        compiler_params=SMALL,
        cost_estimate=CHEAP,
    )(*args)


def gram_kernel(me_ref, codes_ref, own_ref, came_ref, *rest, offs, off, part, mode, last, tensor):
    rest = list(rest)
    came_over = over(rest, *offs)
    partner_ref, far_ref, side_ref, doc_ref, token_ref = rest[:5]
    rest = rest[5:]
    held = [rest.pop(0) for _ in range({"first": 0, "next": 1, "score": 3}[mode])]
    out_ref, rows_ref, cols_ref, acc_ref, doc_sem, sems, role_sems = rest
    me = me_ref[0]
    inner = is_inner(me)
    rows = own_ref.shape[1]
    width = rows_ref.shape[1]
    docs = pltpu.make_async_copy(doc_ref.at[0, :, pl.ds(off, width)], cols_ref, doc_sem.at[0])
    docs.start()

    def slot(k):
        return rows_ref.at[pl.ds(k * rows, rows), :]

    copies = Copies(sems)
    for r in range(CAP):
        copies.start(cut(own_ref, codes_ref[SLOTS + r], off, width), slot(r))
    for k in range(4 * CAP):
        copies.start(side_ref.at[k], slot(4 * CAP + k))

    @pl.when(inner == 1)
    def _():
        more = Copies(role_sems)
        for r in range(CAP):
            more.start(cut(came_ref, codes_ref[SLOTS + CAP + r], 0, width), slot(CAP + r))
        for k in range(2 * CAP, 4 * CAP):
            entry(more, codes_ref[SLOTS + k], came_over, width, slot(k))
        more.wait()

    @pl.when(inner == 0)
    def _():
        more = Copies(role_sems)
        for r in range(CAP):
            more.start(cut(partner_ref, part * 2 * CAP + r, 0, width), slot(CAP + r))
        for k in range(2 * CAP):
            more.start(cut(far_ref, k, 0, width), slot(2 * CAP + k))
        more.wait()

    copies.wait()
    docs.wait()
    step = 256
    if mode == "score":
        acc_ref[...] = held[2][...]

    def block(n, _):
        at = pl.ds(pl.multiple_of(n * step, step), step)
        part = lax.dot_general(
            rows_ref[...], cols_ref[at, :], (((1,), (1,)), ((), ())), preferred_element_type=jnp.float32
        )
        if mode == "first":
            out_ref[:, at] = part
        elif mode == "next":
            out_ref[:, at] = held[0][:, at] + part
        else:
            both = part * (held[0][:, at] + held[1][:, at])
            acc_ref[...] += jnp.sum(both.reshape(8 * CAP, rows, step), axis=1)
        return 0

    lax.fori_loop(0, SEQ_D // step, block, 0)
    if mode == "score" and not last:
        out_ref[...] = acc_ref[...]
    if last:
        total = jnp.sum(acc_ref[...], axis=1, keepdims=True)
        near = jnp.where(inner == 1, me ^ 6, me ^ 4)
        far = jnp.where(inner == 1, me ^ 4, me ^ 6)
        for k, owner in enumerate((me, me ^ 2, near, far, me ^ 1, me ^ 3, near ^ 1, far ^ 1)):
            for t in range(tensor):
                out_ref[owner * tensor + t] = jnp.broadcast_to(total[k * CAP : (k + 1) * CAP], (CAP, 128))


def gram_call(me, codes, own, came, arrays, offs, partner, far, side, doc, off, part, token, mode, held,
              last, tensor):
    late = arrays[-2]
    rows, width = late.shape[1:]
    tokens = doc.shape[1]
    total = 8 * CAP * rows
    args = [me, codes, own, came, *arrays, partner, far, side, doc, token]
    if last:
        out = jax.ShapeDtypeStruct((8 * tensor, CAP, 128), jnp.float32)
    elif mode == "score":
        out = jax.ShapeDtypeStruct((8 * CAP, 256), jnp.float32)
    else:
        out = jax.ShapeDtypeStruct((total, tokens), jnp.float32)
    return pl.pallas_call(
        functools.partial(gram_kernel, offs=offs, off=off, part=part, mode=mode, last=last, tensor=tensor),
        out_shape=out,
        in_specs=[SMEM, SMEM] + [ANY] * (len(args) - 2) + [VMEM] * len(held),
        out_specs=VMEM,
        scratch_shapes=[
            pltpu.VMEM((total, width), doc.dtype),
            pltpu.VMEM((tokens, width), doc.dtype),
            pltpu.VMEM((8 * CAP, 256), jnp.float32),
            pltpu.SemaphoreType.DMA((1,)),
            pltpu.SemaphoreType.DMA((5 * CAP,)),
            pltpu.SemaphoreType.DMA((3 * CAP,)),
        ],
        compiler_params=pltpu.CompilerParams(vmem_limit_bytes=16 * 1024 * 1024),
        cost_estimate=CHEAP,
    )(*args, *held)


def finish_kernel(came_ref, place_ref, out_ref, *, tensor):
    factor = 1.0 / jnp.sqrt(jnp.float32(FF) * jnp.float32(D) * jnp.float32(SEQ_S) * jnp.float32(SEQ_D))
    for p in range(8 * CAP):
        slot = place_ref[p]
        doc, r = slot // CAP, slot % CAP
        total = came_ref[doc * tensor, r, 0]
        for t in range(1, tensor):
            total = total + came_ref[doc * tensor + t, r, 0]
        out_ref[p] = total * factor


def chain(sample_act, sample_grad, doc_act, doc_grad, pair_doc, pair_sample):
    groups, tensor = lax.axis_size("groups"), lax.axis_size("tensor")
    me = jnp.stack([lax.axis_index("docs"), lax.axis_index("groups")]).astype(jnp.int32)
    chunks = [(True, 0, CHUNK), (True, CHUNK, CHUNK)] + [(False, i * CHUNK, CHUNK) for i in range(5)]
    chunks.append((False, 5 * CHUNK, sample_act.shape[2] - 5 * CHUNK))
    total = len(chunks)
    send = lambda x, pairs: lax.ppermute(x, "docs", pairs)
    tab, place, own, z, across = start_call(me, pair_doc, pair_sample, sample_grad, sample_act)
    z0 = send(z, OVER_Z)
    early_grad = send(across, ACROSS)
    z, across = second_call(me, tab, own, sample_grad, sample_act, z)
    z1 = send(z, OVER_Z)
    early_act = send(across, ACROSS)
    tables = lax.all_to_all(
        jnp.broadcast_to(tab[None, :], (groups * 8, 8 * CAP)), ("groups", "docs"), 0, 0, tiled=True
    )
    codes = codes_call(me, tables, groups)

    def send_extras(count):
        if count == 0:
            return tuple(jnp.zeros((EXTRAS[-1],) + x.shape[1:], x.dtype) for x in (sample_grad, sample_act))
        sent = [send(x, ACROSS) for x in ahead_call(count, own, sample_grad, sample_act)]
        return tuple(jnp.pad(x, ((0, EXTRAS[-1] - count), (0, 0), (0, 0))) for x in sent)

    extras = lax.switch(codes[BRANCH], [functools.partial(send_extras, c) for c in EXTRAS])

    ahead_of = [z0, z1]
    main, late, sides = {}, {}, {}
    state = dict(grads=None, score=None)

    def came(i):
        return ahead_of[i] if i < LEAD else main[i - LEAD]

    def sample(i):
        return sample_grad if chunks[i][0] else sample_act

    def over_arrays(i):
        is_grad, off, _ = chunks[i]
        extra = extras[0 if is_grad else 1]
        if i >= LEAD:
            return [late[i], extra], (None, off)
        return [early_grad if is_grad else early_act, late[i], extra], (off, off)

    def mix(i, token):
        _, off, w = chunks[i]
        first = OWN if i < LEAD else 0
        out = mix_call(me, codes, sample(i), came(i), MAIN - first, first, off, w, token)
        late[i] = send(out, ACROSS)
        return out

    def forward(i, token):
        ahead = chunks[i + LEAD][1:] if i + LEAD < total else None
        out = forward_call(me, codes, *over_arrays(i), sample_act, ahead, token)
        main[i] = send(out, OVER_Z)
        return out

    def side(i, token):
        out = side_call(me, codes, tab, sample(i), came(i), *over_arrays(i), ahead_of[i // 2], main[i],
                        chunks[i][1], i % 2, token)
        sides[i] = send(out, OVER_Y)
        return out

    def gram(i, token):
        is_grad, off, w = chunks[i]
        last = i == total - 1
        if is_grad:
            held = [] if i == 0 else [state["grads"]]
            mode = "next" if held else "first"
        else:
            held, mode = [*state["grads"], state["score"]], "score"
        out = gram_call(
            me, codes, sample(i), came(i), *over_arrays(i), ahead_of[i // 2], main[i],
            sides[i], doc_grad if is_grad else doc_act, off, i % 2, token, mode, held, last, tensor,
        )
        if not is_grad:
            state["score"] = out
        elif chunks[i + 1][0]:
            state["grads"] = out
        else:
            state["grads"] = (out, lax.psum(out, "tensor") - out if tensor != 2 else lax.ppermute(
                out, "tensor", [(0, 1), (1, 0)]
            ))
            state["score"] = jnp.zeros((8 * CAP, 256), jnp.float32)
        return out

    token = mix(0, codes)
    z2, z3 = third_call(me, tab, sample_act, token)
    ahead_of.append(send(z2, OVER_Z))
    ahead_of.append(send(z3, OVER_Z))
    token = z2
    for i in range(total + 2):
        if i + 1 < total:
            token = mix(i + 1, token)
        if i < total:
            token = forward(i, token)
        if i >= 2:
            token = gram(i - 2, token)
        if 1 <= i < total + 1:
            token = side(i - 1, token)
    back = lax.all_to_all(state["score"], ("docs", "tensor"), 0, 0, tiled=True)
    return pl.pallas_call(
        functools.partial(finish_kernel, tensor=tensor),
        out_shape=jax.ShapeDtypeStruct((8 * CAP,), jnp.float32),
        in_specs=[SMEM, SMEM],
        out_specs=SMEM,
        compiler_params=SMALL,
        cost_estimate=CHEAP,
    )(back, place)


def codes_kernel(me_ref, all_ref, out_ref, scratch, masks, *, groups):
    group, me = me_ref[1], me_ref[0]
    base = group * 8

    def owner_mask(row, _):
        first = jnp.where((row & 7) < 4, 8, 0)
        mask = jnp.int32(0)
        for j in range(8):
            mask = mask | jnp.left_shift(1, all_ref[row, first + j])
        masks[row] = mask
        return 0

    lax.fori_loop(0, groups * 8, owner_mask, 0)

    def longest(k, best):
        row = (k >> 2) * 8 + 2 + (k & 3)
        return jnp.maximum(best, jnp.maximum(bits(masks[row]), OWN) + bits(masks[row ^ 2]))

    best = lax.fori_loop(0, groups * 4, longest, jnp.int32(0))
    branch = jnp.int32(0)
    for c in EXTRAS[:-1]:
        branch = branch + (best > MAIN + c).astype(jnp.int32)
    for i in range(CODES):
        out_ref[i] = 0
    for i in range(32):
        scratch[i] = 0
    out_ref[BRANCH] = branch
    inner = is_inner(me)
    mine, partner = masks[base + me], masks[base + (me ^ 2)]
    count = jnp.int32(0)
    for s in range(8):
        hit = (mine >> s) & 1
        scratch[jnp.where(hit == 1, count, 31)] = s
        count = count + hit
    count = jnp.maximum(count, OWN)
    for s in range(8):
        hit = (partner >> s) & 1
        scratch[jnp.where(hit == 1, count, 31)] = 8 + s
        count = count + hit
    need = jnp.maximum(count - MAIN, 0)
    for k in range(MAIN):
        out_ref[LIST + k] = scratch[k if k < OWN else k + need]
    far, far_outer = masks[base + (me ^ 6)], masks[base + (me ^ 4)]
    after = jnp.maximum(bits(far), OWN)
    extra = jnp.maximum(after + bits(far_outer) - MAIN, 0)

    def place(near, doc, r):
        owner = base + ((me ^ 6) if near else (me ^ 4))
        sample = all_ref[owner, doc * CAP + r]
        below = jnp.left_shift(1, sample) - 1
        if near:
            at = bits(far & below)
            at = jnp.where(at < OWN, at, jnp.where(at < OWN + extra, at - OWN + SENT, at - extra))
        else:
            at = after + bits(far_outer & below) - extra
        return at * inner

    for r in range(CAP):
        out_ref[STRAIGHT + r] = place(True, me ^ 2, r)
        out_ref[STRAIGHT + CAP + r] = place(False, me ^ 2, r)
        out_ref[DIAG + r] = place(True, me ^ 3, r)
        out_ref[DIAG + CAP + r] = place(False, me ^ 3, r)
        out_ref[SIDE + r] = all_ref[base + (me ^ 2), (me ^ 1) * CAP + r]
        out_ref[SIDE + CAP + r] = place(True, me ^ 1, r)
        out_ref[SIDE + 2 * CAP + r] = place(False, me ^ 1, r)
        out_ref[SLOTS + r] = all_ref[base + me, me * CAP + r]
        out_ref[SLOTS + CAP + r] = all_ref[base + (me ^ 2), me * CAP + r]
        out_ref[SLOTS + 2 * CAP + r] = place(True, me, r)
        out_ref[SLOTS + 3 * CAP + r] = place(False, me, r)


def codes_call(me, tables, groups):
    return pl.pallas_call(
        functools.partial(codes_kernel, groups=groups),
        out_shape=jax.ShapeDtypeStruct((CODES,), jnp.int32),
        in_specs=[SMEM, SMEM],
        out_specs=SMEM,
        scratch_shapes=[pltpu.SMEM((32,), jnp.int32), pltpu.SMEM((groups * 8,), jnp.int32)],
        compiler_params=SMALL,
        cost_estimate=CHEAP,
    )(me, tables)


def direct(sample_act, sample_grad, doc_act, doc_grad, pair_doc, pair_sample):
    owners = lax.axis_size("docs")
    pair_count = pair_doc.shape[0]
    slot_count = owners * CAP
    factor = 1.0 / jnp.sqrt(
        jnp.float32(FF) * jnp.float32(D) * jnp.float32(SEQ_S) * jnp.float32(SEQ_D)
    )
    target = pair_doc[:, 0]
    order = jnp.arange(pair_count, dtype=jnp.int32)
    earlier = (target[:, None] == target[None, :]) & (order[None, :] < order[:, None])
    rank = jnp.sum(earlier.astype(jnp.int32), axis=1)
    slot_of_pair = target * CAP + rank
    chosen = (jnp.arange(slot_count, dtype=jnp.int32)[:, None] == slot_of_pair[None, :]).astype(
        jnp.int32
    )
    slot_sample = jnp.sum(chosen * pair_sample[None, :], axis=1)
    send_act = sample_act[slot_sample]
    send_grad = sample_grad[slot_sample]
    send_act = send_act.reshape(owners, CAP, send_act.shape[1], send_act.shape[2])
    send_grad = send_grad.reshape(owners, CAP, send_grad.shape[1], send_grad.shape[2])
    grad_in = lax.all_to_all(send_grad, "docs", split_axis=0, concat_axis=0, tiled=True)
    act_in = lax.all_to_all(send_act, "docs", split_axis=0, concat_axis=0, tiled=True)
    grad_gram = jnp.einsum("nmsf,tf->nmst", grad_in, doc_grad[0], preferred_element_type=jnp.float32)
    grad_sum = lax.psum(grad_gram, "tensor")
    act_gram = jnp.einsum("nmsf,tf->nmst", act_in, doc_act[0], preferred_element_type=jnp.float32)
    scores = lax.psum(jnp.sum(act_gram * grad_sum, axis=(2, 3)) * factor, "tensor")
    returned = lax.all_to_all(scores, "docs", split_axis=0, concat_axis=0, tiled=True)
    flat_scores = returned.reshape(slot_count)
    return jnp.sum(jnp.where(chosen > 0, flat_scores[:, None], 0.0), axis=0)


def solution(mesh):
    in_specs = (
        P(("groups", "docs"), None, "tensor"),
        P(("groups", "docs"), None, "tensor"),
        P(("groups", "docs"), None, "tensor"),
        P(("groups", "docs"), None, "tensor"),
        P(("groups", "docs"), None),
        P(("groups", "docs")),
    )
    out_specs = P(("groups", "docs"))

    def per_device(sample_act, sample_grad, doc_act, doc_grad, pair_doc, pair_sample):
        fits = (
            mesh.shape["docs"] == 8
            and mesh.shape["tensor"] == 2
            and pair_doc.shape[0] == 8 * CAP
            and sample_act.shape[0] == 8
            and sample_grad.shape[2] == 2 * CHUNK
            and 5 * CHUNK < sample_act.shape[2] <= 6 * CHUNK
        )
        run = chain if fits else direct
        return run(sample_act, sample_grad, doc_act, doc_grad, pair_doc, pair_sample)

    return jax.shard_map(
        per_device, mesh=mesh, in_specs=in_specs, out_specs=out_specs, check_vma=False
    )
```

```python
import functools

import jax
import jax.numpy as jnp
from jax import lax
from jax.experimental import pallas as pl
from jax.experimental.pallas import tpu as pltpu
from jax.sharding import PartitionSpec as P

FF = 11008
D = 4096
SEQ_S = 32
SEQ_D = 768
CAP = 2

ANY = pl.BlockSpec(memory_space=pl.ANY)
SMEM = pl.BlockSpec(memory_space=pltpu.SMEM)
VMEM = pl.BlockSpec(memory_space=pltpu.VMEM)

INNER = (2, 3, 4, 5)
ACROSS = [(i, i ^ 6) for i in INNER]
OVER_Z = [(i, i ^ 2) for i in range(8)]
OVER_Y = [(i, i ^ 1) for i in range(8)]

OWN = 4
MAIN = 12
EXTRAS = (0, 1, 2, 4)

LIST, STRAIGHT, DIAG, SIDE, SLOTS, BRANCH, CODES = 0, 16, 20, 24, 32, 48, 64
SENT = 16


def is_inner(me):
    return ((me >> 1) ^ (me >> 2)) & 1


def bits(mask):
    total = mask & 1
    for i in range(1, 8):
        total = total + ((mask >> i) & 1)
    return total


SMALL = pltpu.CompilerParams(vmem_limit_bytes=6 * 1024 * 1024)
CHEAP = pl.CostEstimate(flops=0, bytes_accessed=1024, transcendentals=0)
CHUNK = 1024
WIDTHS = (1024, 1024, 1024, 1024, 768)
LEAD = 4


class Copies:
    def __init__(self, sems):
        self.sems, self.used, self.held = sems, 0, []

    def start(self, src, dst):
        copy = pltpu.make_async_copy(src, dst, self.sems.at[self.used])
        copy.start()
        self.used += 1
        self.held.append(copy)

    def either(self, first, src, other, dst):
        sem = self.sems.at[self.used]

        @pl.when(first)
        def _():
            pltpu.make_async_copy(src, dst, sem).start()

        @pl.when(jnp.logical_not(first))
        def _():
            pltpu.make_async_copy(other, dst, sem).start()

        self.used += 1
        self.held.append(pltpu.make_async_copy(src, dst, sem))

    def wait(self):
        for copy in self.held:
            copy.wait()
        self.held = []


def cut(ref, i, off, width):
    return ref.at[i, :, pl.ds(off, width)]


def own_slots(sems, inner, me, tab_ref, here, ahead, dst, first):
    @pl.when(inner == 1)
    def _():
        c = Copies(sems)
        for part, (ref, off, width) in enumerate(here):
            for k in range(2 * CAP):
                sample = tab_ref[(me ^ (2 + k // CAP)) * CAP + k % CAP]
                c.start(cut(ref, sample, off, width), cut(dst, first + part * 2 * CAP + k, 0, width))
        c.wait()

    @pl.when(inner == 0)
    def _():
        c = Copies(sems)
        ref, off, width = ahead
        for s in range(8):
            c.start(cut(ref, s, off, width), cut(dst, first + s, 0, width))
        c.wait()


def start_kernel(me_ref, doc_ref, sample_ref, grad_ref, act_ref, tab_ref, place_ref, own_ref, z_ref, across_ref,
                 seen, sems, out_sems):
    me = me_ref[0]
    inner = is_inner(me)
    for d in range(8):
        seen[d] = 0
    for i in range(8 * CAP):
        tab_ref[i] = 0
    for i in range(16):
        own_ref[i] = 0
    mask = jnp.int32(0)
    half = me >> 2
    for p in range(8 * CAP):
        doc = doc_ref[p, 0]
        slot = doc * CAP + jnp.minimum(seen[doc], CAP - 1)
        seen[doc] = seen[doc] + 1
        place_ref[p] = slot
        tab_ref[slot] = sample_ref[p]
        bit = jnp.left_shift(1, sample_ref[p])
        mask = jnp.where((doc >> 2) != half, mask | bit, mask)
    count = jnp.int32(0)
    for s in range(8):
        hit = (mask >> s) & 1
        own_ref[jnp.where(hit == 1, count, 8)] = s
        count = count + hit
    width = grad_ref.shape[2] // 2
    lists = Copies(sems)
    for k in range(OWN):
        lists.start(cut(grad_ref, own_ref[k], 0, 2 * width), across_ref.at[k])
    own_slots(out_sems, inner, me, tab_ref,
              ((grad_ref, 0, width), (grad_ref, width, width)), (grad_ref, 0, width), z_ref, 0)
    lists.wait()


def start_call(me, pair_doc, pair_sample, grad, act):
    rows, width = grad.shape[1:]
    table = jax.ShapeDtypeStruct((16,), jnp.int32)
    return pl.pallas_call(
        start_kernel,
        out_shape=(table, table, table, jax.ShapeDtypeStruct((8, rows, CHUNK), grad.dtype),
                   jax.ShapeDtypeStruct((OWN, rows, width), grad.dtype)),
        in_specs=[SMEM, SMEM, SMEM, ANY, ANY],
        out_specs=(SMEM, SMEM, SMEM, VMEM, VMEM),
        scratch_shapes=[pltpu.SMEM((8,), jnp.int32), pltpu.SemaphoreType.DMA((OWN,)),
                        pltpu.SemaphoreType.DMA((8,))],
        compiler_params=SMALL,
        cost_estimate=CHEAP,
    )(me, pair_doc, pair_sample, grad, act)


def ahead_block_kernel(me_ref, tab_ref, act_ref, far_ref, token_ref, z_ref, sems, *, here, ahead):
    me = me_ref[0]
    own_slots(sems, is_inner(me), me, tab_ref, [(act_ref, *span) for span in here], (far_ref, *ahead), z_ref, 0)


def ahead_block_call(me, tab, act, far, token, here, ahead):
    return pl.pallas_call(
        functools.partial(ahead_block_kernel, here=here, ahead=ahead),
        out_shape=jax.ShapeDtypeStruct((8, act.shape[1], CHUNK), act.dtype),
        in_specs=[SMEM, SMEM, ANY, ANY, ANY],
        out_specs=VMEM,
        scratch_shapes=[pltpu.SemaphoreType.DMA((8,))],
        compiler_params=SMALL,
        cost_estimate=CHEAP,
    )(me, tab, act, far, token)


def mix_kernel(me_ref, codes_ref, own_ref, came_ref, token_ref, list_ref, sems, *, first, off, at):
    count, _, width = list_ref.shape

    @pl.when(is_inner(me_ref[0]) == 1)
    def _():
        copies = Copies(sems)
        for k in range(count):
            code = codes_ref[LIST + first + k]
            mine = code < 8
            copies.either(mine, cut(own_ref, jnp.minimum(code, 7), off, width),
                          cut(came_ref, at + jnp.maximum(code - 8, 0), 0, width), list_ref.at[k])
        copies.wait()


def mix_call(me, codes, own, came, at, count, first, off, width, token):
    rows = own.shape[1]
    return pl.pallas_call(
        functools.partial(mix_kernel, first=first, off=off, at=at),
        out_shape=jax.ShapeDtypeStruct((count, rows, width), own.dtype),
        in_specs=[SMEM, SMEM, ANY, ANY, ANY],
        out_specs=VMEM,
        scratch_shapes=[pltpu.SemaphoreType.DMA((count,))],
        compiler_params=SMALL,
        cost_estimate=CHEAP,
    )(me, codes, own, came, token)


def entry(copies, code, came_over, width, dst):
    early, late_ref, (extra_ref, extra_off) = came_over
    sem = copies.sems.at[copies.used]
    copies.used += 1
    skip = 0 if early is None else OWN

    @pl.when(code >= SENT)
    def _():
        pltpu.make_async_copy(cut(extra_ref, jnp.maximum(code - SENT, 0), extra_off, width), dst, sem).start()

    @pl.when((code >= skip) & (code < SENT))
    def _():
        at = jnp.clip(code - skip, 0, late_ref.shape[0] - 1)
        pltpu.make_async_copy(cut(late_ref, at, 0, width), dst, sem).start()

    if early is not None:
        @pl.when(code < OWN)
        def _():
            pltpu.make_async_copy(cut(early[0], jnp.minimum(code, OWN - 1), early[1], width), dst, sem).start()

    copies.held.append(pltpu.make_async_copy(cut(late_ref, 0, 0, width), dst, sem))


def over(rest, early_off, extra_off):
    early = None if early_off is None else (rest.pop(0), early_off)
    return early, rest.pop(0), (rest.pop(0), extra_off)


def blank_kernel(token_ref, *refs):
    pass


def blank_call(shapes, token):
    return tuple(pl.pallas_call(
        blank_kernel,
        out_shape=[jax.ShapeDtypeStruct(x, jnp.bfloat16) for x in shapes],
        in_specs=[SMEM],
        out_specs=[ANY] * len(shapes),
        compiler_params=SMALL,
        cost_estimate=CHEAP,
    )(token))


def ahead_kernel(own_ref, grad_ref, act_ref, grad_out, act_out, sems):
    copies = Copies(sems)
    for k in range(grad_out.shape[0]):
        copies.start(grad_ref.at[own_ref[OWN + k]], grad_out.at[k])
        copies.start(act_ref.at[own_ref[OWN + k]], act_out.at[k])
    copies.wait()


def ahead_call(count, own, grad, act):
    return pl.pallas_call(
        ahead_kernel,
        out_shape=tuple(jax.ShapeDtypeStruct((count,) + x.shape[1:], x.dtype) for x in (grad, act)),
        in_specs=[SMEM, ANY, ANY],
        out_specs=(VMEM, VMEM),
        scratch_shapes=[pltpu.SemaphoreType.DMA((2 * count,))],
        compiler_params=SMALL,
        cost_estimate=CHEAP,
    )(own, grad, act)


def forward_kernel(me_ref, codes_ref, *rest, offs, ahead):
    rest = list(rest)
    came_over = over(rest, *offs)
    ahead_ref, token_ref, z_ref, sems = rest
    inner = is_inner(me_ref[0])
    width = came_over[1].shape[2]

    @pl.when(inner == 1)
    def _():
        copies = Copies(sems)
        for k in range(2 * CAP):
            entry(copies, codes_ref[STRAIGHT + k], came_over, width, cut(z_ref, k, 0, width))
            entry(copies, codes_ref[DIAG + k], came_over, width, cut(z_ref, 2 * CAP + k, 0, width))
        copies.wait()

    if ahead is not None:
        @pl.when(inner == 0)
        def _():
            copies = Copies(sems)
            off, some = ahead
            for s in range(8):
                copies.start(cut(ahead_ref, s, off, some), cut(z_ref, s, 0, some))
            copies.wait()


def forward_call(me, codes, arrays, offs, ahead_array, ahead, token):
    late = arrays[-2]
    rows, width = late.shape[1:]
    args = [me, codes, *arrays, ahead_array, token]
    return pl.pallas_call(
        functools.partial(forward_kernel, offs=offs, ahead=ahead),
        out_shape=jax.ShapeDtypeStruct((8, rows, width), late.dtype),
        in_specs=[SMEM, SMEM] + [ANY] * (len(args) - 2),
        out_specs=VMEM,
        scratch_shapes=[pltpu.SemaphoreType.DMA((8,))],
        compiler_params=SMALL,
        cost_estimate=CHEAP,
    )(*args)


def side_kernel(me_ref, codes_ref, tab_ref, sample_ref, came_ref, *rest, offs, off, at, part):
    rest = list(rest)
    came_over = over(rest, *offs)
    own_ref, far_ref, token_ref, side_ref, sems, role_sems = rest
    me = me_ref[0]
    inner = is_inner(me)
    width = side_ref.shape[2]
    mine = Copies(sems)
    for r in range(CAP):
        mine.start(cut(sample_ref, tab_ref[(me ^ 1) * CAP + r], off, width), side_ref.at[r])

    @pl.when(inner == 1)
    def _():
        copies = Copies(role_sems)
        for k in range(CAP):
            copies.start(cut(came_ref, at + codes_ref[SIDE + k], 0, width), side_ref.at[CAP + k])
        for k in range(CAP, 3 * CAP):
            entry(copies, codes_ref[SIDE + k], came_over, width, side_ref.at[CAP + k])
        copies.wait()

    @pl.when(inner == 0)
    def _():
        copies = Copies(role_sems)
        for k in range(CAP):
            copies.start(cut(own_ref, part + CAP + k, 0, width), side_ref.at[CAP + k])
        for k in range(2 * CAP):
            copies.start(cut(far_ref, 2 * CAP + k, 0, width), side_ref.at[2 * CAP + k])
        copies.wait()

    mine.wait()


def side_call(me, codes, tab, sample, came, at, arrays, offs, own, part, far, off, token):
    late = arrays[-2]
    rows, width = late.shape[1:]
    args = [me, codes, tab, sample, came, *arrays, own, far, token]
    return pl.pallas_call(
        functools.partial(side_kernel, offs=offs, off=off, at=at, part=part),
        out_shape=jax.ShapeDtypeStruct((4 * CAP, rows, width), late.dtype),
        in_specs=[SMEM, SMEM, SMEM] + [ANY] * (len(args) - 3),
        out_specs=VMEM,
        scratch_shapes=[pltpu.SemaphoreType.DMA((CAP,)), pltpu.SemaphoreType.DMA((3 * CAP,))],
        compiler_params=SMALL,
        cost_estimate=CHEAP,
    )(*args)


def gram_kernel(me_ref, codes_ref, own_ref, came_ref, *rest, offs, off, at, part, mode, last, tensor):
    rest = list(rest)
    came_over = over(rest, *offs)
    partner_ref, far_ref, side_ref, doc_ref, token_ref = rest[:5]
    rest = rest[5:]
    held = [rest.pop(0) for _ in range({"first": 0, "next": 1, "score": 3}[mode])]
    out_ref, rows_ref, cols_ref, acc_ref, doc_sem, sems, role_sems = rest
    me = me_ref[0]
    inner = is_inner(me)
    rows = own_ref.shape[1]
    width = rows_ref.shape[1]
    docs = pltpu.make_async_copy(doc_ref.at[0, :, pl.ds(off, width)], cols_ref, doc_sem.at[0])
    docs.start()

    def slot(k):
        return rows_ref.at[pl.ds(k * rows, rows), :]

    copies = Copies(sems)
    for r in range(CAP):
        copies.start(cut(own_ref, codes_ref[SLOTS + r], off, width), slot(r))
    for k in range(4 * CAP):
        copies.start(side_ref.at[k], slot(4 * CAP + k))

    @pl.when(inner == 1)
    def _():
        more = Copies(role_sems)
        for r in range(CAP):
            more.start(cut(came_ref, at + codes_ref[SLOTS + CAP + r], 0, width), slot(CAP + r))
        for k in range(2 * CAP, 4 * CAP):
            entry(more, codes_ref[SLOTS + k], came_over, width, slot(k))
        more.wait()

    @pl.when(inner == 0)
    def _():
        more = Copies(role_sems)
        for r in range(CAP):
            more.start(cut(partner_ref, part + r, 0, width), slot(CAP + r))
        for k in range(2 * CAP):
            more.start(cut(far_ref, k, 0, width), slot(2 * CAP + k))
        more.wait()

    copies.wait()
    docs.wait()
    step = 256
    if mode == "score":
        acc_ref[...] = held[2][...]

    def block(n, _):
        cols = pl.ds(pl.multiple_of(n * step, step), step)
        gram = lax.dot_general(
            rows_ref[...], cols_ref[cols, :], (((1,), (1,)), ((), ())), preferred_element_type=jnp.float32
        )
        if mode == "first":
            out_ref[:, cols] = gram
        elif mode == "next":
            out_ref[:, cols] = held[0][:, cols] + gram
        else:
            both = gram * (held[0][:, cols] + held[1][:, cols])
            acc_ref[...] += jnp.sum(both.reshape(8 * CAP, rows, step), axis=1)
        return 0

    lax.fori_loop(0, SEQ_D // step, block, 0)
    if mode == "score" and not last:
        out_ref[...] = acc_ref[...]
    if last:
        total = jnp.sum(acc_ref[...], axis=1, keepdims=True)
        near = jnp.where(inner == 1, me ^ 6, me ^ 4)
        far = jnp.where(inner == 1, me ^ 4, me ^ 6)
        for k, owner in enumerate((me, me ^ 2, near, far, me ^ 1, me ^ 3, near ^ 1, far ^ 1)):
            for t in range(tensor):
                out_ref[owner * tensor + t] = jnp.broadcast_to(total[k * CAP : (k + 1) * CAP], (CAP, 128))


def gram_call(me, codes, own, came, at, arrays, offs, partner, part, far, side, doc, off, token, mode, held,
              last, tensor):
    late = arrays[-2]
    rows, width = late.shape[1:]
    tokens = doc.shape[1]
    total = 8 * CAP * rows
    args = [me, codes, own, came, *arrays, partner, far, side, doc, token]
    if last:
        out = jax.ShapeDtypeStruct((8 * tensor, CAP, 128), jnp.float32)
    elif mode == "score":
        out = jax.ShapeDtypeStruct((8 * CAP, 256), jnp.float32)
    else:
        out = jax.ShapeDtypeStruct((total, tokens), jnp.float32)
    return pl.pallas_call(
        functools.partial(gram_kernel, offs=offs, off=off, at=at, part=part, mode=mode, last=last, tensor=tensor),
        out_shape=out,
        in_specs=[SMEM, SMEM] + [ANY] * (len(args) - 2) + [VMEM] * len(held),
        out_specs=VMEM,
        scratch_shapes=[
            pltpu.VMEM((total, width), doc.dtype),
            pltpu.VMEM((tokens, width), doc.dtype),
            pltpu.VMEM((8 * CAP, 256), jnp.float32),
            pltpu.SemaphoreType.DMA((1,)),
            pltpu.SemaphoreType.DMA((5 * CAP,)),
            pltpu.SemaphoreType.DMA((3 * CAP,)),
        ],
        compiler_params=pltpu.CompilerParams(vmem_limit_bytes=16 * 1024 * 1024),
        cost_estimate=CHEAP,
    )(*args, *held)


def finish_kernel(came_ref, place_ref, out_ref, *, tensor):
    factor = 1.0 / jnp.sqrt(jnp.float32(FF) * jnp.float32(D) * jnp.float32(SEQ_S) * jnp.float32(SEQ_D))
    for p in range(8 * CAP):
        slot = place_ref[p]
        doc, r = slot // CAP, slot % CAP
        total = came_ref[doc * tensor, r, 0]
        for t in range(1, tensor):
            total = total + came_ref[doc * tensor + t, r, 0]
        out_ref[p] = total * factor


def chain(sample_act, sample_grad, doc_act, doc_grad, pair_doc, pair_sample):
    groups, tensor = lax.axis_size("groups"), lax.axis_size("tensor")
    me = jnp.stack([lax.axis_index("docs"), lax.axis_index("groups")]).astype(jnp.int32)
    chunks = [(True, 0, CHUNK), (True, CHUNK, CHUNK)]
    off = 0
    for w in WIDTHS:
        chunks.append((False, off, w))
        off += w
    chunks.append((False, off, sample_act.shape[2] - off))
    total = len(chunks)
    send = lambda x, pairs: lax.ppermute(x, "docs", pairs)
    tab, place, own, z, across = start_call(me, pair_doc, pair_sample, sample_grad, sample_act)
    z0 = send(z, OVER_Z)
    early_grad = send(across, ACROSS)
    tables = lax.all_to_all(
        jnp.broadcast_to(tab[None, :], (groups * 8, 8 * CAP)), ("groups", "docs"), 0, 0, tiled=True
    )
    codes = codes_call(me, tables, groups)
    listed = list_call(me, tab, tables, early_grad)

    def send_extras(count):
        if count == 0:
            return blank_call([(EXTRAS[-1],) + x.shape[1:] for x in (sample_grad, sample_act)], own)
        sent = [send(x, ACROSS) for x in ahead_call(count, own, sample_grad, sample_act)]
        return tuple(jnp.pad(x, ((0, EXTRAS[-1] - count), (0, 0), (0, 0))) for x in sent)

    extras = lax.switch(codes[BRANCH], [functools.partial(send_extras, c) for c in EXTRAS])

    ahead_of = [(z0, 0)]
    main, late, sides = {}, {}, {}
    state = dict(grads=None, score=None)

    def came(i):
        return ahead_of[i] if i < LEAD else (main[i - LEAD], 0)

    def partner(i):
        array, first = ahead_of[i // 2]
        return array, first + i % 2 * 2 * CAP

    def sample(i):
        return sample_grad if chunks[i][0] else sample_act

    def over_arrays(i):
        is_grad, off, _ = chunks[i]
        extra = extras[0 if is_grad else 1]
        if not is_grad:
            return [late[i], extra], (None, off)
        return [early_grad, late[i], extra], (off, off)

    def mix(i, token):
        _, off, w = chunks[i]
        first = OWN if chunks[i][0] else 0
        out = mix_call(me, listed, sample(i), *came(i), MAIN - first, first, off, w, token)
        late[i] = send(out, ACROSS)
        return out

    def forward(i, token):
        ahead = chunks[i + LEAD][1:] if i + LEAD < total else None
        out = forward_call(me, codes, *over_arrays(i), sample_act, ahead, token)
        main[i] = send(out, OVER_Z)
        return out

    def side(i, token):
        out = side_call(me, codes, tab, sample(i), *came(i), *over_arrays(i), *partner(i), main[i], chunks[i][1],
                        token)
        sides[i] = send(out, OVER_Y)
        return out

    def gram(i, token):
        is_grad, off, w = chunks[i]
        last = i == total - 1
        if is_grad:
            held = [] if i == 0 else [state["grads"]]
            mode = "next" if held else "first"
        else:
            held, mode = [*state["grads"], state["score"]], "score"
        out = gram_call(
            me, codes, sample(i), *came(i), *over_arrays(i), *partner(i), main[i], sides[i],
            doc_grad if is_grad else doc_act, off, token, mode, held, last, tensor,
        )
        if not is_grad:
            state["score"] = out
        elif chunks[i + 1][0]:
            state["grads"] = out
        else:
            state["grads"] = (out, lax.psum(out, "tensor") - out if tensor != 2 else lax.ppermute(
                out, "tensor", [(0, 1), (1, 0)]
            ))
            state["score"] = jnp.zeros((8 * CAP, 256), jnp.float32)
        return out

    token = mix(0, listed)
    spans = [c[1:] for c in chunks[2:]]

    def ahead_block(i, token):
        out = ahead_block_call(me, tab, sample_act, sample(i), token, spans[2 * i - 2 : 2 * i], chunks[i][1:])
        ahead_of.append((send(out, OVER_Z), 0))
        return out

    token = ahead_block(1, token)
    token = ahead_block(2, token)
    for i in range(total + 2):
        if i + 1 < total:
            token = mix(i + 1, token)
        if i < total:
            token = forward(i, token)
        if i == 0:
            token = ahead_block(3, token)
        if 1 <= i < total + 1:
            token = side(i - 1, token)
        if i >= 2:
            token = gram(i - 2, token)
    back = lax.all_to_all(state["score"], ("docs", "tensor"), 0, 0, tiled=True)
    return pl.pallas_call(
        functools.partial(finish_kernel, tensor=tensor),
        out_shape=jax.ShapeDtypeStruct((8 * CAP,), jnp.float32),
        in_specs=[SMEM, SMEM],
        out_specs=SMEM,
        compiler_params=SMALL,
        cost_estimate=CHEAP,
    )(back, place)


def list_kernel(me_ref, mine_ref, all_ref, token_ref, out_ref, scratch):
    me = me_ref[0]
    first = jnp.where(me < 4, 8, 0)
    mine, partner = jnp.int32(0), jnp.int32(0)
    for j in range(8):
        mine = mine | jnp.left_shift(1, mine_ref[first + j])
        partner = partner | jnp.left_shift(1, all_ref[me_ref[1] * 8 + (me ^ 2), first + j])
    for i in range(32):
        scratch[i] = 0
    for i in range(16):
        out_ref[i] = 0
    count = jnp.int32(0)
    for s in range(8):
        hit = (mine >> s) & 1
        scratch[jnp.where(hit == 1, count, 31)] = s
        count = count + hit
    count = jnp.maximum(count, OWN)
    for s in range(8):
        hit = (partner >> s) & 1
        scratch[jnp.where(hit == 1, count, 31)] = 8 + s
        count = count + hit
    need = jnp.maximum(count - MAIN, 0)
    for k in range(MAIN):
        out_ref[LIST + k] = scratch[k if k < OWN else k + need]


def list_call(me, mine, tables, token):
    return pl.pallas_call(
        list_kernel,
        out_shape=jax.ShapeDtypeStruct((16,), jnp.int32),
        in_specs=[SMEM, SMEM, SMEM, ANY],
        out_specs=SMEM,
        scratch_shapes=[pltpu.SMEM((32,), jnp.int32)],
        compiler_params=SMALL,
        cost_estimate=CHEAP,
    )(me, mine, tables, token)


def codes_kernel(me_ref, all_ref, out_ref, masks, *, groups):
    group, me = me_ref[1], me_ref[0]
    base = group * 8

    def owner_mask(row, _):
        first = jnp.where((row & 7) < 4, 8, 0)
        mask = jnp.int32(0)
        for j in range(8):
            mask = mask | jnp.left_shift(1, all_ref[row, first + j])
        masks[row] = mask
        return 0

    lax.fori_loop(0, groups * 8, owner_mask, 0)

    def longest(k, best):
        row = (k >> 2) * 8 + 2 + (k & 3)
        return jnp.maximum(best, jnp.maximum(bits(masks[row]), OWN) + bits(masks[row ^ 2]))

    best = lax.fori_loop(0, groups * 4, longest, jnp.int32(0))
    branch = jnp.int32(0)
    for c in EXTRAS[:-1]:
        branch = branch + (best > MAIN + c).astype(jnp.int32)
    for i in range(CODES):
        out_ref[i] = 0
    out_ref[BRANCH] = branch
    inner = is_inner(me)
    far, far_outer = masks[base + (me ^ 6)], masks[base + (me ^ 4)]
    after = jnp.maximum(bits(far), OWN)
    extra = jnp.maximum(after + bits(far_outer) - MAIN, 0)

    def place(near, doc, r):
        owner = base + ((me ^ 6) if near else (me ^ 4))
        sample = all_ref[owner, doc * CAP + r]
        below = jnp.left_shift(1, sample) - 1
        if near:
            at = bits(far & below)
            at = jnp.where(at < OWN, at, jnp.where(at < OWN + extra, at - OWN + SENT, at - extra))
        else:
            at = after + bits(far_outer & below) - extra
        return at * inner

    for r in range(CAP):
        out_ref[STRAIGHT + r] = place(True, me ^ 2, r)
        out_ref[STRAIGHT + CAP + r] = place(False, me ^ 2, r)
        out_ref[DIAG + r] = place(True, me ^ 3, r)
        out_ref[DIAG + CAP + r] = place(False, me ^ 3, r)
        out_ref[SIDE + r] = all_ref[base + (me ^ 2), (me ^ 1) * CAP + r]
        out_ref[SIDE + CAP + r] = place(True, me ^ 1, r)
        out_ref[SIDE + 2 * CAP + r] = place(False, me ^ 1, r)
        out_ref[SLOTS + r] = all_ref[base + me, me * CAP + r]
        out_ref[SLOTS + CAP + r] = all_ref[base + (me ^ 2), me * CAP + r]
        out_ref[SLOTS + 2 * CAP + r] = place(True, me, r)
        out_ref[SLOTS + 3 * CAP + r] = place(False, me, r)


def codes_call(me, tables, groups):
    return pl.pallas_call(
        functools.partial(codes_kernel, groups=groups),
        out_shape=jax.ShapeDtypeStruct((CODES,), jnp.int32),
        in_specs=[SMEM, SMEM],
        out_specs=SMEM,
        scratch_shapes=[pltpu.SMEM((groups * 8,), jnp.int32)],
        compiler_params=SMALL,
        cost_estimate=CHEAP,
    )(me, tables)


def direct(sample_act, sample_grad, doc_act, doc_grad, pair_doc, pair_sample):
    owners = lax.axis_size("docs")
    pair_count = pair_doc.shape[0]
    slot_count = owners * CAP
    factor = 1.0 / jnp.sqrt(
        jnp.float32(FF) * jnp.float32(D) * jnp.float32(SEQ_S) * jnp.float32(SEQ_D)
    )
    target = pair_doc[:, 0]
    order = jnp.arange(pair_count, dtype=jnp.int32)
    earlier = (target[:, None] == target[None, :]) & (order[None, :] < order[:, None])
    rank = jnp.sum(earlier.astype(jnp.int32), axis=1)
    slot_of_pair = target * CAP + rank
    chosen = (jnp.arange(slot_count, dtype=jnp.int32)[:, None] == slot_of_pair[None, :]).astype(
        jnp.int32
    )
    slot_sample = jnp.sum(chosen * pair_sample[None, :], axis=1)
    send_act = sample_act[slot_sample]
    send_grad = sample_grad[slot_sample]
    send_act = send_act.reshape(owners, CAP, send_act.shape[1], send_act.shape[2])
    send_grad = send_grad.reshape(owners, CAP, send_grad.shape[1], send_grad.shape[2])
    grad_in = lax.all_to_all(send_grad, "docs", split_axis=0, concat_axis=0, tiled=True)
    act_in = lax.all_to_all(send_act, "docs", split_axis=0, concat_axis=0, tiled=True)
    grad_gram = jnp.einsum("nmsf,tf->nmst", grad_in, doc_grad[0], preferred_element_type=jnp.float32)
    grad_sum = lax.psum(grad_gram, "tensor")
    act_gram = jnp.einsum("nmsf,tf->nmst", act_in, doc_act[0], preferred_element_type=jnp.float32)
    scores = lax.psum(jnp.sum(act_gram * grad_sum, axis=(2, 3)) * factor, "tensor")
    returned = lax.all_to_all(scores, "docs", split_axis=0, concat_axis=0, tiled=True)
    flat_scores = returned.reshape(slot_count)
    return jnp.sum(jnp.where(chosen > 0, flat_scores[:, None], 0.0), axis=0)


def solution(mesh):
    in_specs = (
        P(("groups", "docs"), None, "tensor"),
        P(("groups", "docs"), None, "tensor"),
        P(("groups", "docs"), None, "tensor"),
        P(("groups", "docs"), None, "tensor"),
        P(("groups", "docs"), None),
        P(("groups", "docs")),
    )
    out_specs = P(("groups", "docs"))

    def per_device(sample_act, sample_grad, doc_act, doc_grad, pair_doc, pair_sample):
        fits = (
            mesh.shape["docs"] == 8
            and mesh.shape["tensor"] == 2
            and pair_doc.shape[0] == 8 * CAP
            and sample_act.shape[0] == 8
            and sample_grad.shape[2] == 2 * CHUNK
            and 0 < sample_act.shape[2] - sum(WIDTHS) <= CHUNK
            and sample_act.shape[2] % 128 == 0
        )
        run = chain if fits else direct
        return run(sample_act, sample_grad, doc_act, doc_grad, pair_doc, pair_sample)

    return jax.shard_map(
        per_device, mesh=mesh, in_specs=in_specs, out_specs=out_specs, check_vma=False
    )
```

```python
import functools

import jax
import jax.numpy as jnp
from jax import lax
from jax.experimental import pallas as pl
from jax.experimental.pallas import tpu as pltpu
from jax.sharding import PartitionSpec as P

FF = 11008
D = 4096
SEQ_S = 32
SEQ_D = 768
CAP = 2

ANY = pl.BlockSpec(memory_space=pl.ANY)
SMEM = pl.BlockSpec(memory_space=pltpu.SMEM)
VMEM = pl.BlockSpec(memory_space=pltpu.VMEM)

INNER = (2, 3, 4, 5)
ACROSS = [(i, i ^ 6) for i in INNER]
OVER_Z = [(i, i ^ 2) for i in range(8)]
OVER_Y = [(i, i ^ 1) for i in range(8)]

OWN = 4
MAIN = 12
EXTRAS = (0, 1, 2, 4)

LIST, STRAIGHT, DIAG, SIDE, SLOTS, BRANCH, CODES = 0, 16, 20, 24, 32, 48, 64
SENT = 16


def is_inner(me):
    return ((me >> 1) ^ (me >> 2)) & 1


def bits(mask):
    total = mask & 1
    for i in range(1, 8):
        total = total + ((mask >> i) & 1)
    return total


SMALL = pltpu.CompilerParams(vmem_limit_bytes=6 * 1024 * 1024)
CHEAP = pl.CostEstimate(flops=0, bytes_accessed=1024, transcendentals=0)
CHUNK = 1024
WIDTHS = (1024, 1024, 1024, 1024, 768)
LEAD = 4


class Copies:
    def __init__(self, sems):
        self.sems, self.used, self.held = sems, 0, []

    def start(self, src, dst):
        copy = pltpu.make_async_copy(src, dst, self.sems.at[self.used])
        copy.start()
        self.used += 1
        self.held.append(copy)

    def either(self, first, src, other, dst):
        sem = self.sems.at[self.used]

        @pl.when(first)
        def _():
            pltpu.make_async_copy(src, dst, sem).start()

        @pl.when(jnp.logical_not(first))
        def _():
            pltpu.make_async_copy(other, dst, sem).start()

        self.used += 1
        self.held.append(pltpu.make_async_copy(src, dst, sem))

    def wait(self):
        for copy in self.held:
            copy.wait()
        self.held = []


def cut(ref, i, off, width):
    return ref.at[i, :, pl.ds(off, width)]


def own_slots(sems, inner, me, tab_ref, here, ahead, dst, first):
    @pl.when(inner == 1)
    def _():
        c = Copies(sems)
        for part, (ref, off, width) in enumerate(here):
            for k in range(2 * CAP):
                sample = tab_ref[(me ^ (2 + k // CAP)) * CAP + k % CAP]
                c.start(cut(ref, sample, off, width), cut(dst, first + part * 2 * CAP + k, 0, width))
        c.wait()

    @pl.when(inner == 0)
    def _():
        c = Copies(sems)
        ref, off, width = ahead
        for s in range(8):
            c.start(cut(ref, s, off, width), cut(dst, first + s, 0, width))
        c.wait()


def start_kernel(me_ref, doc_ref, sample_ref, grad_ref, act_ref, tab_ref, place_ref, own_ref, z_ref, across_ref,
                 seen, sems, out_sems):
    me = me_ref[0]
    inner = is_inner(me)
    for d in range(8):
        seen[d] = 0
    for i in range(8 * CAP):
        tab_ref[i] = 0
    for i in range(16):
        own_ref[i] = 0
    mask = jnp.int32(0)
    half = me >> 2
    for p in range(8 * CAP):
        doc = doc_ref[p, 0]
        slot = doc * CAP + jnp.minimum(seen[doc], CAP - 1)
        seen[doc] = seen[doc] + 1
        place_ref[p] = slot
        tab_ref[slot] = sample_ref[p]
        bit = jnp.left_shift(1, sample_ref[p])
        mask = jnp.where((doc >> 2) != half, mask | bit, mask)
    count = jnp.int32(0)
    for s in range(8):
        hit = (mask >> s) & 1
        own_ref[jnp.where(hit == 1, count, 8)] = s
        count = count + hit
    width = grad_ref.shape[2] // 2
    lists = Copies(sems)
    for k in range(OWN):
        lists.start(cut(grad_ref, own_ref[k], 0, 2 * width), across_ref.at[k])
    own_slots(out_sems, inner, me, tab_ref,
              ((grad_ref, 0, width), (grad_ref, width, width)), (grad_ref, 0, width), z_ref, 0)
    lists.wait()


def start_call(me, pair_doc, pair_sample, grad, act):
    rows, width = grad.shape[1:]
    table = jax.ShapeDtypeStruct((16,), jnp.int32)
    return pl.pallas_call(
        start_kernel,
        out_shape=(table, table, table, jax.ShapeDtypeStruct((8, rows, CHUNK), grad.dtype),
                   jax.ShapeDtypeStruct((OWN, rows, width), grad.dtype)),
        in_specs=[SMEM, SMEM, SMEM, ANY, ANY],
        out_specs=(SMEM, SMEM, SMEM, VMEM, VMEM),
        scratch_shapes=[pltpu.SMEM((8,), jnp.int32), pltpu.SemaphoreType.DMA((OWN,)),
                        pltpu.SemaphoreType.DMA((8,))],
        compiler_params=SMALL,
        cost_estimate=CHEAP,
    )(me, pair_doc, pair_sample, grad, act)


def ahead_block_kernel(me_ref, tab_ref, act_ref, far_ref, token_ref, z_ref, sems, *, here, ahead):
    me = me_ref[0]
    own_slots(sems, is_inner(me), me, tab_ref, [(act_ref, *span) for span in here], (far_ref, *ahead), z_ref, 0)


def ahead_block_call(me, tab, act, far, token, here, ahead):
    return pl.pallas_call(
        functools.partial(ahead_block_kernel, here=here, ahead=ahead),
        out_shape=jax.ShapeDtypeStruct((8, act.shape[1], CHUNK), act.dtype),
        in_specs=[SMEM, SMEM, ANY, ANY, ANY],
        out_specs=VMEM,
        scratch_shapes=[pltpu.SemaphoreType.DMA((8,))],
        compiler_params=SMALL,
        cost_estimate=CHEAP,
    )(me, tab, act, far, token)


def mix_kernel(me_ref, codes_ref, own_ref, came_ref, token_ref, list_ref, sems, *, first, off, at):
    count, _, width = list_ref.shape

    @pl.when(is_inner(me_ref[0]) == 1)
    def _():
        copies = Copies(sems)
        for k in range(count):
            code = codes_ref[LIST + first + k]
            mine = code < 8
            copies.either(mine, cut(own_ref, jnp.minimum(code, 7), off, width),
                          cut(came_ref, at + jnp.maximum(code - 8, 0), 0, width), list_ref.at[k])
        copies.wait()


def mix_call(me, codes, own, came, at, count, first, off, width, token):
    rows = own.shape[1]
    return pl.pallas_call(
        functools.partial(mix_kernel, first=first, off=off, at=at),
        out_shape=jax.ShapeDtypeStruct((count, rows, width), own.dtype),
        in_specs=[SMEM, SMEM, ANY, ANY, ANY],
        out_specs=VMEM,
        scratch_shapes=[pltpu.SemaphoreType.DMA((count,))],
        compiler_params=SMALL,
        cost_estimate=CHEAP,
    )(me, codes, own, came, token)


def entry(copies, code, came_over, width, dst):
    early, late_ref, (extra_ref, extra_off) = came_over
    sem = copies.sems.at[copies.used]
    copies.used += 1
    skip = 0 if early is None else OWN

    @pl.when(code >= SENT)
    def _():
        pltpu.make_async_copy(cut(extra_ref, jnp.maximum(code - SENT, 0), extra_off, width), dst, sem).start()

    @pl.when((code >= skip) & (code < SENT))
    def _():
        at = jnp.clip(code - skip, 0, late_ref.shape[0] - 1)
        pltpu.make_async_copy(cut(late_ref, at, 0, width), dst, sem).start()

    if early is not None:
        @pl.when(code < OWN)
        def _():
            pltpu.make_async_copy(cut(early[0], jnp.minimum(code, OWN - 1), early[1], width), dst, sem).start()

    copies.held.append(pltpu.make_async_copy(cut(late_ref, 0, 0, width), dst, sem))


def over(rest, early_off, extra_off):
    early = None if early_off is None else (rest.pop(0), early_off)
    return early, rest.pop(0), (rest.pop(0), extra_off)


def blank_kernel(token_ref, *refs):
    pass


def blank_call(shapes, token):
    return tuple(pl.pallas_call(
        blank_kernel,
        out_shape=[jax.ShapeDtypeStruct(x, jnp.bfloat16) for x in shapes],
        in_specs=[SMEM],
        out_specs=[ANY] * len(shapes),
        compiler_params=SMALL,
        cost_estimate=CHEAP,
    )(token))


def ahead_kernel(own_ref, grad_ref, act_ref, grad_out, act_out, sems):
    copies = Copies(sems)
    for k in range(grad_out.shape[0]):
        copies.start(grad_ref.at[own_ref[OWN + k]], grad_out.at[k])
        copies.start(act_ref.at[own_ref[OWN + k]], act_out.at[k])
    copies.wait()


def ahead_call(count, own, grad, act):
    return pl.pallas_call(
        ahead_kernel,
        out_shape=tuple(jax.ShapeDtypeStruct((count,) + x.shape[1:], x.dtype) for x in (grad, act)),
        in_specs=[SMEM, ANY, ANY],
        out_specs=(VMEM, VMEM),
        scratch_shapes=[pltpu.SemaphoreType.DMA((2 * count,))],
        compiler_params=SMALL,
        cost_estimate=CHEAP,
    )(own, grad, act)


def forward_kernel(me_ref, codes_ref, *rest, offs, ahead):
    rest = list(rest)
    came_over = over(rest, *offs)
    ahead_ref, token_ref, z_ref, sems = rest
    inner = is_inner(me_ref[0])
    width = came_over[1].shape[2]

    @pl.when(inner == 1)
    def _():
        copies = Copies(sems)
        for k in range(2 * CAP):
            entry(copies, codes_ref[STRAIGHT + k], came_over, width, cut(z_ref, k, 0, width))
            entry(copies, codes_ref[DIAG + k], came_over, width, cut(z_ref, 2 * CAP + k, 0, width))
        copies.wait()

    if ahead is not None:
        @pl.when(inner == 0)
        def _():
            copies = Copies(sems)
            off, some = ahead
            for s in range(8):
                copies.start(cut(ahead_ref, s, off, some), cut(z_ref, s, 0, some))
            copies.wait()


def forward_call(me, codes, arrays, offs, ahead_array, ahead, token):
    late = arrays[-2]
    rows, width = late.shape[1:]
    args = [me, codes, *arrays, ahead_array, token]
    return pl.pallas_call(
        functools.partial(forward_kernel, offs=offs, ahead=ahead),
        out_shape=jax.ShapeDtypeStruct((8, rows, width), late.dtype),
        in_specs=[SMEM, SMEM] + [ANY] * (len(args) - 2),
        out_specs=VMEM,
        scratch_shapes=[pltpu.SemaphoreType.DMA((8,))],
        compiler_params=SMALL,
        cost_estimate=CHEAP,
    )(*args)


def side_kernel(me_ref, codes_ref, tab_ref, sample_ref, came_ref, *rest, offs, off, at, part):
    rest = list(rest)
    came_over = over(rest, *offs)
    own_ref, far_ref, token_ref, side_ref, sems, role_sems = rest
    me = me_ref[0]
    inner = is_inner(me)
    width = side_ref.shape[2]
    mine = Copies(sems)
    for r in range(CAP):
        mine.start(cut(sample_ref, tab_ref[(me ^ 1) * CAP + r], off, width), side_ref.at[r])

    @pl.when(inner == 1)
    def _():
        copies = Copies(role_sems)
        for k in range(CAP):
            copies.start(cut(came_ref, at + codes_ref[SIDE + k], 0, width), side_ref.at[CAP + k])
        for k in range(CAP, 3 * CAP):
            entry(copies, codes_ref[SIDE + k], came_over, width, side_ref.at[CAP + k])
        copies.wait()

    @pl.when(inner == 0)
    def _():
        copies = Copies(role_sems)
        for k in range(CAP):
            copies.start(cut(own_ref, part + CAP + k, 0, width), side_ref.at[CAP + k])
        for k in range(2 * CAP):
            copies.start(cut(far_ref, 2 * CAP + k, 0, width), side_ref.at[2 * CAP + k])
        copies.wait()

    mine.wait()


def side_call(me, codes, tab, sample, came, at, arrays, offs, own, part, far, off, token):
    late = arrays[-2]
    rows, width = late.shape[1:]
    args = [me, codes, tab, sample, came, *arrays, own, far, token]
    return pl.pallas_call(
        functools.partial(side_kernel, offs=offs, off=off, at=at, part=part),
        out_shape=jax.ShapeDtypeStruct((4 * CAP, rows, width), late.dtype),
        in_specs=[SMEM, SMEM, SMEM] + [ANY] * (len(args) - 3),
        out_specs=VMEM,
        scratch_shapes=[pltpu.SemaphoreType.DMA((CAP,)), pltpu.SemaphoreType.DMA((3 * CAP,))],
        compiler_params=SMALL,
        cost_estimate=CHEAP,
    )(*args)


def gram_kernel(me_ref, codes_ref, own_ref, came_ref, *rest, offs, off, at, part, mode, last, tensor):
    rest = list(rest)
    came_over = over(rest, *offs)
    partner_ref, far_ref, side_ref, doc_ref, token_ref = rest[:5]
    rest = rest[5:]
    held = [rest.pop(0) for _ in range({"first": 0, "next": 1, "score": 3}[mode])]
    out_ref, rows_ref, cols_ref, acc_ref, doc_sem, sems, role_sems = rest
    me = me_ref[0]
    inner = is_inner(me)
    rows = own_ref.shape[1]
    width = rows_ref.shape[1]
    docs = pltpu.make_async_copy(doc_ref.at[0, :, pl.ds(off, width)], cols_ref, doc_sem.at[0])
    docs.start()

    def slot(k):
        return rows_ref.at[pl.ds(k * rows, rows), :]

    copies = Copies(sems)
    for r in range(CAP):
        copies.start(cut(own_ref, codes_ref[SLOTS + r], off, width), slot(r))
    for k in range(4 * CAP):
        copies.start(side_ref.at[k], slot(4 * CAP + k))

    @pl.when(inner == 1)
    def _():
        more = Copies(role_sems)
        for r in range(CAP):
            more.start(cut(came_ref, at + codes_ref[SLOTS + CAP + r], 0, width), slot(CAP + r))
        for k in range(2 * CAP, 4 * CAP):
            entry(more, codes_ref[SLOTS + k], came_over, width, slot(k))
        more.wait()

    @pl.when(inner == 0)
    def _():
        more = Copies(role_sems)
        for r in range(CAP):
            more.start(cut(partner_ref, part + r, 0, width), slot(CAP + r))
        for k in range(2 * CAP):
            more.start(cut(far_ref, k, 0, width), slot(2 * CAP + k))
        more.wait()

    copies.wait()
    docs.wait()
    step = 256
    if mode == "score":
        acc_ref[...] = held[2][...]

    def block(n, _):
        cols = pl.ds(pl.multiple_of(n * step, step), step)
        gram = lax.dot_general(
            rows_ref[...], cols_ref[cols, :], (((1,), (1,)), ((), ())), preferred_element_type=jnp.float32
        )
        if mode == "first":
            out_ref[:, cols] = gram
        elif mode == "next":
            out_ref[:, cols] = held[0][:, cols] + gram
        else:
            both = gram * (held[0][:, cols] + held[1][:, cols])
            acc_ref[...] += jnp.sum(both.reshape(8 * CAP, rows, step), axis=1)
        return 0

    lax.fori_loop(0, SEQ_D // step, block, 0)
    if mode == "score" and not last:
        out_ref[...] = acc_ref[...]
    if last:
        total = jnp.sum(acc_ref[...], axis=1, keepdims=True)
        near = jnp.where(inner == 1, me ^ 6, me ^ 4)
        far = jnp.where(inner == 1, me ^ 4, me ^ 6)
        for k, owner in enumerate((me, me ^ 2, near, far, me ^ 1, me ^ 3, near ^ 1, far ^ 1)):
            for t in range(tensor):
                out_ref[owner * tensor + t] = jnp.broadcast_to(total[k * CAP : (k + 1) * CAP], (CAP, 128))


def gram_call(me, codes, own, came, at, arrays, offs, partner, part, far, side, doc, off, token, mode, held,
              last, tensor):
    late = arrays[-2]
    rows, width = late.shape[1:]
    tokens = doc.shape[1]
    total = 8 * CAP * rows
    args = [me, codes, own, came, *arrays, partner, far, side, doc, token]
    if last:
        out = jax.ShapeDtypeStruct((8 * tensor, CAP, 128), jnp.float32)
    elif mode == "score":
        out = jax.ShapeDtypeStruct((8 * CAP, 256), jnp.float32)
    else:
        out = jax.ShapeDtypeStruct((total, tokens), jnp.float32)
    return pl.pallas_call(
        functools.partial(gram_kernel, offs=offs, off=off, at=at, part=part, mode=mode, last=last, tensor=tensor),
        out_shape=out,
        in_specs=[SMEM, SMEM] + [ANY] * (len(args) - 2) + [VMEM] * len(held),
        out_specs=VMEM,
        scratch_shapes=[
            pltpu.VMEM((total, width), doc.dtype),
            pltpu.VMEM((tokens, width), doc.dtype),
            pltpu.VMEM((8 * CAP, 256), jnp.float32),
            pltpu.SemaphoreType.DMA((1,)),
            pltpu.SemaphoreType.DMA((5 * CAP,)),
            pltpu.SemaphoreType.DMA((3 * CAP,)),
        ],
        compiler_params=pltpu.CompilerParams(vmem_limit_bytes=16 * 1024 * 1024),
        cost_estimate=CHEAP,
    )(*args, *held)


def finish_kernel(came_ref, place_ref, out_ref, *, tensor):
    factor = 1.0 / jnp.sqrt(jnp.float32(FF) * jnp.float32(D) * jnp.float32(SEQ_S) * jnp.float32(SEQ_D))
    for p in range(8 * CAP):
        slot = place_ref[p]
        doc, r = slot // CAP, slot % CAP
        total = came_ref[doc * tensor, r, 0]
        for t in range(1, tensor):
            total = total + came_ref[doc * tensor + t, r, 0]
        out_ref[p] = total * factor


def chain(sample_act, sample_grad, doc_act, doc_grad, pair_doc, pair_sample):
    groups, tensor = lax.axis_size("groups"), lax.axis_size("tensor")
    me = jnp.stack([lax.axis_index("docs"), lax.axis_index("groups")]).astype(jnp.int32)
    chunks = [(True, 0, CHUNK), (True, CHUNK, CHUNK)]
    off = 0
    for w in WIDTHS:
        chunks.append((False, off, w))
        off += w
    chunks.append((False, off, sample_act.shape[2] - off))
    total = len(chunks)
    send = lambda x, pairs: lax.ppermute(x, "docs", pairs)
    tab, place, own, z, across = start_call(me, pair_doc, pair_sample, sample_grad, sample_act)
    z0 = send(z, OVER_Z)
    early_grad = send(across, ACROSS)
    tables = lax.all_to_all(
        jnp.broadcast_to(tab[None, :], (groups * 8, 8 * CAP)), ("groups", "docs"), 0, 0, tiled=True
    )
    codes = codes_call(me, tables, groups)
    listed = list_call(me, tab, tables, early_grad)

    def send_extras(count):
        if count == 0:
            return blank_call([(EXTRAS[-1],) + x.shape[1:] for x in (sample_grad, sample_act)], own)
        sent = [send(x, ACROSS) for x in ahead_call(count, own, sample_grad, sample_act)]
        return tuple(jnp.pad(x, ((0, EXTRAS[-1] - count), (0, 0), (0, 0))) for x in sent)

    extras = lax.switch(codes[BRANCH], [functools.partial(send_extras, c) for c in EXTRAS])

    ahead_of = [(z0, 0)]
    main, late, sides = {}, {}, {}
    state = dict(grads=None, score=None)

    def came(i):
        return ahead_of[i] if i < LEAD else (main[i - LEAD], 0)

    def partner(i):
        array, first = ahead_of[i // 2]
        return array, first + i % 2 * 2 * CAP

    def sample(i):
        return sample_grad if chunks[i][0] else sample_act

    def over_arrays(i):
        is_grad, off, _ = chunks[i]
        extra = extras[0 if is_grad else 1]
        if not is_grad:
            return [late[i], extra], (None, off)
        return [early_grad, late[i], extra], (off, off)

    def mix(i, token):
        _, off, w = chunks[i]
        first = OWN if chunks[i][0] else 0
        out = mix_call(me, listed, sample(i), *came(i), MAIN - first, first, off, w, token)
        late[i] = send(out, ACROSS)
        return out

    def forward(i, token):
        ahead = chunks[i + LEAD][1:] if i + LEAD < total else None
        out = forward_call(me, codes, *over_arrays(i), sample_act, ahead, token)
        main[i] = send(out, OVER_Z)
        return out

    def side(i, token):
        out = side_call(me, codes, tab, sample(i), *came(i), *over_arrays(i), *partner(i), main[i], chunks[i][1],
                        token)
        sides[i] = send(out, OVER_Y)
        return out

    def gram(i, token):
        is_grad, off, w = chunks[i]
        last = i == total - 1
        if is_grad:
            held = [] if i == 0 else [state["grads"]]
            mode = "next" if held else "first"
        else:
            held, mode = [*state["grads"], state["score"]], "score"
        out = gram_call(
            me, codes, sample(i), *came(i), *over_arrays(i), *partner(i), main[i], sides[i],
            doc_grad if is_grad else doc_act, off, token, mode, held, last, tensor,
        )
        if not is_grad:
            state["score"] = out
        elif chunks[i + 1][0]:
            state["grads"] = out
        else:
            state["grads"] = (out, lax.psum(out, "tensor") - out if tensor != 2 else lax.ppermute(
                out, "tensor", [(0, 1), (1, 0)]
            ))
            state["score"] = jnp.zeros((8 * CAP, 256), jnp.float32)
        return out

    token = mix(0, listed)
    spans = [c[1:] for c in chunks[2:]]

    def ahead_block(i, token):
        out = ahead_block_call(me, tab, sample_act, sample(i), token, spans[2 * i - 2 : 2 * i], chunks[i][1:])
        ahead_of.append((send(out, OVER_Z), 0))
        return out

    token = ahead_block(1, token)
    ahead_block(2, token)
    token = extras[0]
    for i in range(total + 2):
        if i + 1 < total:
            token = mix(i + 1, token)
        if i < total:
            token = forward(i, token)
        if i == 0:
            token = ahead_block(3, token)
        if 1 <= i < total + 1:
            token = side(i - 1, token)
        if i >= 2:
            token = gram(i - 2, token)
    back = lax.all_to_all(state["score"], ("docs", "tensor"), 0, 0, tiled=True)
    return pl.pallas_call(
        functools.partial(finish_kernel, tensor=tensor),
        out_shape=jax.ShapeDtypeStruct((8 * CAP,), jnp.float32),
        in_specs=[SMEM, SMEM],
        out_specs=SMEM,
        compiler_params=SMALL,
        cost_estimate=CHEAP,
    )(back, place)


def list_kernel(me_ref, mine_ref, all_ref, token_ref, out_ref, scratch):
    me = me_ref[0]
    first = jnp.where(me < 4, 8, 0)
    mine, partner = jnp.int32(0), jnp.int32(0)
    for j in range(8):
        mine = mine | jnp.left_shift(1, mine_ref[first + j])
        partner = partner | jnp.left_shift(1, all_ref[me_ref[1] * 8 + (me ^ 2), first + j])
    for i in range(32):
        scratch[i] = 0
    for i in range(16):
        out_ref[i] = 0
    count = jnp.int32(0)
    for s in range(8):
        hit = (mine >> s) & 1
        scratch[jnp.where(hit == 1, count, 31)] = s
        count = count + hit
    count = jnp.maximum(count, OWN)
    for s in range(8):
        hit = (partner >> s) & 1
        scratch[jnp.where(hit == 1, count, 31)] = 8 + s
        count = count + hit
    need = jnp.maximum(count - MAIN, 0)
    for k in range(MAIN):
        out_ref[LIST + k] = scratch[k if k < OWN else k + need]


def list_call(me, mine, tables, token):
    return pl.pallas_call(
        list_kernel,
        out_shape=jax.ShapeDtypeStruct((16,), jnp.int32),
        in_specs=[SMEM, SMEM, SMEM, ANY],
        out_specs=SMEM,
        scratch_shapes=[pltpu.SMEM((32,), jnp.int32)],
        compiler_params=SMALL,
        cost_estimate=CHEAP,
    )(me, mine, tables, token)


def codes_kernel(me_ref, all_ref, out_ref, masks, *, groups):
    group, me = me_ref[1], me_ref[0]
    base = group * 8

    def owner_mask(row, _):
        first = jnp.where((row & 7) < 4, 8, 0)
        mask = jnp.int32(0)
        for j in range(8):
            mask = mask | jnp.left_shift(1, all_ref[row, first + j])
        masks[row] = mask
        return 0

    lax.fori_loop(0, groups * 8, owner_mask, 0)

    def longest(k, best):
        row = (k >> 2) * 8 + 2 + (k & 3)
        return jnp.maximum(best, jnp.maximum(bits(masks[row]), OWN) + bits(masks[row ^ 2]))

    best = lax.fori_loop(0, groups * 4, longest, jnp.int32(0))
    branch = jnp.int32(0)
    for c in EXTRAS[:-1]:
        branch = branch + (best > MAIN + c).astype(jnp.int32)
    for i in range(CODES):
        out_ref[i] = 0
    out_ref[BRANCH] = branch
    inner = is_inner(me)
    far, far_outer = masks[base + (me ^ 6)], masks[base + (me ^ 4)]
    after = jnp.maximum(bits(far), OWN)
    extra = jnp.maximum(after + bits(far_outer) - MAIN, 0)

    def place(near, doc, r):
        owner = base + ((me ^ 6) if near else (me ^ 4))
        sample = all_ref[owner, doc * CAP + r]
        below = jnp.left_shift(1, sample) - 1
        if near:
            at = bits(far & below)
            at = jnp.where(at < OWN, at, jnp.where(at < OWN + extra, at - OWN + SENT, at - extra))
        else:
            at = after + bits(far_outer & below) - extra
        return at * inner

    for r in range(CAP):
        out_ref[STRAIGHT + r] = place(True, me ^ 2, r)
        out_ref[STRAIGHT + CAP + r] = place(False, me ^ 2, r)
        out_ref[DIAG + r] = place(True, me ^ 3, r)
        out_ref[DIAG + CAP + r] = place(False, me ^ 3, r)
        out_ref[SIDE + r] = all_ref[base + (me ^ 2), (me ^ 1) * CAP + r]
        out_ref[SIDE + CAP + r] = place(True, me ^ 1, r)
        out_ref[SIDE + 2 * CAP + r] = place(False, me ^ 1, r)
        out_ref[SLOTS + r] = all_ref[base + me, me * CAP + r]
        out_ref[SLOTS + CAP + r] = all_ref[base + (me ^ 2), me * CAP + r]
        out_ref[SLOTS + 2 * CAP + r] = place(True, me, r)
        out_ref[SLOTS + 3 * CAP + r] = place(False, me, r)


def codes_call(me, tables, groups):
    return pl.pallas_call(
        functools.partial(codes_kernel, groups=groups),
        out_shape=jax.ShapeDtypeStruct((CODES,), jnp.int32),
        in_specs=[SMEM, SMEM],
        out_specs=SMEM,
        scratch_shapes=[pltpu.SMEM((groups * 8,), jnp.int32)],
        compiler_params=SMALL,
        cost_estimate=CHEAP,
    )(me, tables)


def direct(sample_act, sample_grad, doc_act, doc_grad, pair_doc, pair_sample):
    owners = lax.axis_size("docs")
    pair_count = pair_doc.shape[0]
    slot_count = owners * CAP
    factor = 1.0 / jnp.sqrt(
        jnp.float32(FF) * jnp.float32(D) * jnp.float32(SEQ_S) * jnp.float32(SEQ_D)
    )
    target = pair_doc[:, 0]
    order = jnp.arange(pair_count, dtype=jnp.int32)
    earlier = (target[:, None] == target[None, :]) & (order[None, :] < order[:, None])
    rank = jnp.sum(earlier.astype(jnp.int32), axis=1)
    slot_of_pair = target * CAP + rank
    chosen = (jnp.arange(slot_count, dtype=jnp.int32)[:, None] == slot_of_pair[None, :]).astype(
        jnp.int32
    )
    slot_sample = jnp.sum(chosen * pair_sample[None, :], axis=1)
    send_act = sample_act[slot_sample]
    send_grad = sample_grad[slot_sample]
    send_act = send_act.reshape(owners, CAP, send_act.shape[1], send_act.shape[2])
    send_grad = send_grad.reshape(owners, CAP, send_grad.shape[1], send_grad.shape[2])
    grad_in = lax.all_to_all(send_grad, "docs", split_axis=0, concat_axis=0, tiled=True)
    act_in = lax.all_to_all(send_act, "docs", split_axis=0, concat_axis=0, tiled=True)
    grad_gram = jnp.einsum("nmsf,tf->nmst", grad_in, doc_grad[0], preferred_element_type=jnp.float32)
    grad_sum = lax.psum(grad_gram, "tensor")
    act_gram = jnp.einsum("nmsf,tf->nmst", act_in, doc_act[0], preferred_element_type=jnp.float32)
    scores = lax.psum(jnp.sum(act_gram * grad_sum, axis=(2, 3)) * factor, "tensor")
    returned = lax.all_to_all(scores, "docs", split_axis=0, concat_axis=0, tiled=True)
    flat_scores = returned.reshape(slot_count)
    return jnp.sum(jnp.where(chosen > 0, flat_scores[:, None], 0.0), axis=0)


def solution(mesh):
    in_specs = (
        P(("groups", "docs"), None, "tensor"),
        P(("groups", "docs"), None, "tensor"),
        P(("groups", "docs"), None, "tensor"),
        P(("groups", "docs"), None, "tensor"),
        P(("groups", "docs"), None),
        P(("groups", "docs")),
    )
    out_specs = P(("groups", "docs"))

    def per_device(sample_act, sample_grad, doc_act, doc_grad, pair_doc, pair_sample):
        fits = (
            mesh.shape["docs"] == 8
            and mesh.shape["tensor"] == 2
            and pair_doc.shape[0] == 8 * CAP
            and sample_act.shape[0] == 8
            and sample_grad.shape[2] == 2 * CHUNK
            and 0 < sample_act.shape[2] - sum(WIDTHS) <= CHUNK
            and sample_act.shape[2] % 128 == 0
        )
        run = chain if fits else direct
        return run(sample_act, sample_grad, doc_act, doc_grad, pair_doc, pair_sample)

    return jax.shard_map(
        per_device, mesh=mesh, in_specs=in_specs, out_specs=out_specs, check_vma=False
    )
```

```python
import functools

import jax
import jax.numpy as jnp
from jax import lax
from jax.experimental import pallas as pl
from jax.experimental.pallas import tpu as pltpu
from jax.sharding import PartitionSpec as P

FF = 11008
D = 4096
SEQ_S = 32
SEQ_D = 768
CAP = 2

ANY = pl.BlockSpec(memory_space=pl.ANY)
SMEM = pl.BlockSpec(memory_space=pltpu.SMEM)
VMEM = pl.BlockSpec(memory_space=pltpu.VMEM)

INNER = (2, 3, 4, 5)
ACROSS = [(i, i ^ 6) for i in INNER]
OVER_Z = [(i, i ^ 2) for i in range(8)]
OVER_Y = [(i, i ^ 1) for i in range(8)]

OWN = 4
MAIN = 12
EXTRAS = (0, 1, 2, 4)

LIST, STRAIGHT, DIAG, SIDE, SLOTS, BRANCH, CODES = 0, 16, 20, 24, 32, 48, 64
SENT = 16


def is_inner(me):
    return ((me >> 1) ^ (me >> 2)) & 1


def bits(mask):
    total = mask & 1
    for i in range(1, 8):
        total = total + ((mask >> i) & 1)
    return total


SMALL = pltpu.CompilerParams(vmem_limit_bytes=6 * 1024 * 1024)
CHEAP = pl.CostEstimate(flops=0, bytes_accessed=1024, transcendentals=0)
CHUNK = 1024
WIDTHS = (1024, 1024, 1024, 1024, 768)
LEAD = 4


class Copies:
    def __init__(self, sems):
        self.sems, self.used, self.held = sems, 0, []

    def start(self, src, dst):
        copy = pltpu.make_async_copy(src, dst, self.sems.at[self.used])
        copy.start()
        self.used += 1
        self.held.append(copy)

    def either(self, first, src, other, dst):
        sem = self.sems.at[self.used]

        @pl.when(first)
        def _():
            pltpu.make_async_copy(src, dst, sem).start()

        @pl.when(jnp.logical_not(first))
        def _():
            pltpu.make_async_copy(other, dst, sem).start()

        self.used += 1
        self.held.append(pltpu.make_async_copy(src, dst, sem))

    def wait(self):
        for copy in self.held:
            copy.wait()
        self.held = []


def cut(ref, i, off, width):
    return ref.at[i, :, pl.ds(off, width)]


def own_slots(sems, inner, me, tab_ref, here, ahead, dst, first):
    @pl.when(inner == 1)
    def _():
        c = Copies(sems)
        for part, (ref, off, width) in enumerate(here):
            for k in range(2 * CAP):
                sample = tab_ref[(me ^ (2 + k // CAP)) * CAP + k % CAP]
                c.start(cut(ref, sample, off, width), cut(dst, first + part * 2 * CAP + k, 0, width))
        c.wait()

    @pl.when(inner == 0)
    def _():
        c = Copies(sems)
        ref, off, width = ahead
        for s in range(8):
            c.start(cut(ref, s, off, width), cut(dst, first + s, 0, width))
        c.wait()


def start_kernel(me_ref, doc_ref, sample_ref, grad_ref, act_ref, tab_ref, place_ref, own_ref, z_ref, across_ref,
                 seen, sems, out_sems):
    me = me_ref[0]
    inner = is_inner(me)
    for d in range(8):
        seen[d] = 0
    for i in range(8 * CAP):
        tab_ref[i] = 0
    for i in range(16):
        own_ref[i] = 0
    mask = jnp.int32(0)
    half = me >> 2
    for p in range(8 * CAP):
        doc = doc_ref[p, 0]
        slot = doc * CAP + jnp.minimum(seen[doc], CAP - 1)
        seen[doc] = seen[doc] + 1
        place_ref[p] = slot
        tab_ref[slot] = sample_ref[p]
        bit = jnp.left_shift(1, sample_ref[p])
        mask = jnp.where((doc >> 2) != half, mask | bit, mask)
    count = jnp.int32(0)
    for s in range(8):
        hit = (mask >> s) & 1
        own_ref[jnp.where(hit == 1, count, 8)] = s
        count = count + hit
    width = grad_ref.shape[2] // 2
    lists = Copies(sems)
    for k in range(OWN):
        lists.start(cut(grad_ref, own_ref[k], 0, 2 * width), across_ref.at[k])
    own_slots(out_sems, inner, me, tab_ref,
              ((grad_ref, 0, width), (grad_ref, width, width)), (grad_ref, 0, width), z_ref, 0)
    lists.wait()


def start_call(me, pair_doc, pair_sample, grad, act):
    rows, width = grad.shape[1:]
    table = jax.ShapeDtypeStruct((16,), jnp.int32)
    return pl.pallas_call(
        start_kernel,
        out_shape=(table, table, table, jax.ShapeDtypeStruct((8, rows, CHUNK), grad.dtype),
                   jax.ShapeDtypeStruct((OWN, rows, width), grad.dtype)),
        in_specs=[SMEM, SMEM, SMEM, ANY, ANY],
        out_specs=(SMEM, SMEM, SMEM, VMEM, VMEM),
        scratch_shapes=[pltpu.SMEM((8,), jnp.int32), pltpu.SemaphoreType.DMA((OWN,)),
                        pltpu.SemaphoreType.DMA((8,))],
        compiler_params=SMALL,
        cost_estimate=CHEAP,
    )(me, pair_doc, pair_sample, grad, act)


def ahead_block_kernel(me_ref, tab_ref, act_ref, far_ref, token_ref, z_ref, sems, *, here, ahead):
    me = me_ref[0]
    own_slots(sems, is_inner(me), me, tab_ref, [(act_ref, *span) for span in here], (far_ref, *ahead), z_ref, 0)


def ahead_block_call(me, tab, act, far, token, here, ahead):
    return pl.pallas_call(
        functools.partial(ahead_block_kernel, here=here, ahead=ahead),
        out_shape=jax.ShapeDtypeStruct((8, act.shape[1], CHUNK), act.dtype),
        in_specs=[SMEM, SMEM, ANY, ANY, ANY],
        out_specs=VMEM,
        scratch_shapes=[pltpu.SemaphoreType.DMA((8,))],
        compiler_params=SMALL,
        cost_estimate=CHEAP,
    )(me, tab, act, far, token)


def mix_kernel(me_ref, codes_ref, own_ref, came_ref, token_ref, list_ref, sems, *, first, off, at):
    count, _, width = list_ref.shape

    @pl.when(is_inner(me_ref[0]) == 1)
    def _():
        copies = Copies(sems)
        for k in range(count):
            code = codes_ref[LIST + first + k]
            mine = code < 8
            copies.either(mine, cut(own_ref, jnp.minimum(code, 7), off, width),
                          cut(came_ref, at + jnp.maximum(code - 8, 0), 0, width), list_ref.at[k])
        copies.wait()


def mix_call(me, codes, own, came, at, count, first, off, width, token):
    rows = own.shape[1]
    return pl.pallas_call(
        functools.partial(mix_kernel, first=first, off=off, at=at),
        out_shape=jax.ShapeDtypeStruct((count, rows, width), own.dtype),
        in_specs=[SMEM, SMEM, ANY, ANY, ANY],
        out_specs=VMEM,
        scratch_shapes=[pltpu.SemaphoreType.DMA((count,))],
        compiler_params=SMALL,
        cost_estimate=CHEAP,
    )(me, codes, own, came, token)


def entry(copies, code, came_over, width, dst):
    early, late_ref, (extra_ref, extra_off) = came_over
    sem = copies.sems.at[copies.used]
    copies.used += 1
    skip = 0 if early is None else OWN

    @pl.when(code >= SENT)
    def _():
        pltpu.make_async_copy(cut(extra_ref, jnp.maximum(code - SENT, 0), extra_off, width), dst, sem).start()

    @pl.when((code >= skip) & (code < SENT))
    def _():
        at = jnp.clip(code - skip, 0, late_ref.shape[0] - 1)
        pltpu.make_async_copy(cut(late_ref, at, 0, width), dst, sem).start()

    if early is not None:
        @pl.when(code < OWN)
        def _():
            pltpu.make_async_copy(cut(early[0], jnp.minimum(code, OWN - 1), early[1], width), dst, sem).start()

    copies.held.append(pltpu.make_async_copy(cut(late_ref, 0, 0, width), dst, sem))


def over(rest, early_off, extra_off):
    early = None if early_off is None else (rest.pop(0), early_off)
    return early, rest.pop(0), (rest.pop(0), extra_off)


def blank_kernel(token_ref, *refs):
    pass


def blank_call(shapes, token):
    return tuple(pl.pallas_call(
        blank_kernel,
        out_shape=[jax.ShapeDtypeStruct(x, jnp.bfloat16) for x in shapes],
        in_specs=[SMEM],
        out_specs=[ANY] * len(shapes),
        compiler_params=SMALL,
        cost_estimate=CHEAP,
    )(token))


def ahead_kernel(own_ref, grad_ref, act_ref, grad_out, act_out, sems):
    copies = Copies(sems)
    for k in range(grad_out.shape[0]):
        copies.start(grad_ref.at[own_ref[OWN + k]], grad_out.at[k])
        copies.start(act_ref.at[own_ref[OWN + k]], act_out.at[k])
    copies.wait()


def ahead_call(count, own, grad, act):
    return pl.pallas_call(
        ahead_kernel,
        out_shape=tuple(jax.ShapeDtypeStruct((count,) + x.shape[1:], x.dtype) for x in (grad, act)),
        in_specs=[SMEM, ANY, ANY],
        out_specs=(VMEM, VMEM),
        scratch_shapes=[pltpu.SemaphoreType.DMA((2 * count,))],
        compiler_params=SMALL,
        cost_estimate=CHEAP,
    )(own, grad, act)


def forward_kernel(me_ref, codes_ref, *rest, offs, ahead):
    rest = list(rest)
    came_over = over(rest, *offs)
    ahead_ref, token_ref, z_ref, sems = rest
    inner = is_inner(me_ref[0])
    width = came_over[1].shape[2]

    @pl.when(inner == 1)
    def _():
        copies = Copies(sems)
        for k in range(2 * CAP):
            entry(copies, codes_ref[STRAIGHT + k], came_over, width, cut(z_ref, k, 0, width))
            entry(copies, codes_ref[DIAG + k], came_over, width, cut(z_ref, 2 * CAP + k, 0, width))
        copies.wait()

    if ahead is not None:
        @pl.when(inner == 0)
        def _():
            copies = Copies(sems)
            off, some = ahead
            for s in range(8):
                copies.start(cut(ahead_ref, s, off, some), cut(z_ref, s, 0, some))
            copies.wait()


def forward_call(me, codes, arrays, offs, ahead_array, ahead, token):
    late = arrays[-2]
    rows, width = late.shape[1:]
    args = [me, codes, *arrays, ahead_array, token]
    return pl.pallas_call(
        functools.partial(forward_kernel, offs=offs, ahead=ahead),
        out_shape=jax.ShapeDtypeStruct((8, rows, width), late.dtype),
        in_specs=[SMEM, SMEM] + [ANY] * (len(args) - 2),
        out_specs=VMEM,
        scratch_shapes=[pltpu.SemaphoreType.DMA((8,))],
        compiler_params=SMALL,
        cost_estimate=CHEAP,
    )(*args)


def side_kernel(me_ref, codes_ref, tab_ref, sample_ref, came_ref, *rest, offs, off, at, part):
    rest = list(rest)
    came_over = over(rest, *offs)
    own_ref, far_ref, token_ref, side_ref, sems, role_sems = rest
    me = me_ref[0]
    inner = is_inner(me)
    width = side_ref.shape[2]
    mine = Copies(sems)
    for r in range(CAP):
        mine.start(cut(sample_ref, tab_ref[(me ^ 1) * CAP + r], off, width), side_ref.at[r])

    @pl.when(inner == 1)
    def _():
        copies = Copies(role_sems)
        for k in range(CAP):
            copies.start(cut(came_ref, at + codes_ref[SIDE + k], 0, width), side_ref.at[CAP + k])
        for k in range(CAP, 3 * CAP):
            entry(copies, codes_ref[SIDE + k], came_over, width, side_ref.at[CAP + k])
        copies.wait()

    @pl.when(inner == 0)
    def _():
        copies = Copies(role_sems)
        for k in range(CAP):
            copies.start(cut(own_ref, part + CAP + k, 0, width), side_ref.at[CAP + k])
        for k in range(2 * CAP):
            copies.start(cut(far_ref, 2 * CAP + k, 0, width), side_ref.at[2 * CAP + k])
        copies.wait()

    mine.wait()


def side_call(me, codes, tab, sample, came, at, arrays, offs, own, part, far, off, token):
    late = arrays[-2]
    rows, width = late.shape[1:]
    args = [me, codes, tab, sample, came, *arrays, own, far, token]
    return pl.pallas_call(
        functools.partial(side_kernel, offs=offs, off=off, at=at, part=part),
        out_shape=jax.ShapeDtypeStruct((4 * CAP, rows, width), late.dtype),
        in_specs=[SMEM, SMEM, SMEM] + [ANY] * (len(args) - 3),
        out_specs=VMEM,
        scratch_shapes=[pltpu.SemaphoreType.DMA((CAP,)), pltpu.SemaphoreType.DMA((3 * CAP,))],
        compiler_params=SMALL,
        cost_estimate=CHEAP,
    )(*args)


def gram_kernel(me_ref, codes_ref, own_ref, came_ref, *rest, offs, off, at, part, mode, last, tensor):
    rest = list(rest)
    came_over = over(rest, *offs)
    partner_ref, far_ref, side_ref, doc_ref, token_ref = rest[:5]
    rest = rest[5:]
    held = [rest.pop(0) for _ in range({"first": 0, "next": 1, "score": 3}[mode])]
    out_ref, rows_ref, cols_ref, acc_ref, doc_sem, sems, role_sems = rest
    me = me_ref[0]
    inner = is_inner(me)
    rows = own_ref.shape[1]
    width = rows_ref.shape[1]
    docs = pltpu.make_async_copy(doc_ref.at[0, :, pl.ds(off, width)], cols_ref, doc_sem.at[0])
    docs.start()

    def slot(k):
        return rows_ref.at[pl.ds(k * rows, rows), :]

    copies = Copies(sems)
    for r in range(CAP):
        copies.start(cut(own_ref, codes_ref[SLOTS + r], off, width), slot(r))
    for k in range(4 * CAP):
        copies.start(side_ref.at[k], slot(4 * CAP + k))

    @pl.when(inner == 1)
    def _():
        more = Copies(role_sems)
        for r in range(CAP):
            more.start(cut(came_ref, at + codes_ref[SLOTS + CAP + r], 0, width), slot(CAP + r))
        for k in range(2 * CAP, 4 * CAP):
            entry(more, codes_ref[SLOTS + k], came_over, width, slot(k))
        more.wait()

    @pl.when(inner == 0)
    def _():
        more = Copies(role_sems)
        for r in range(CAP):
            more.start(cut(partner_ref, part + r, 0, width), slot(CAP + r))
        for k in range(2 * CAP):
            more.start(cut(far_ref, k, 0, width), slot(2 * CAP + k))
        more.wait()

    copies.wait()
    docs.wait()
    step = 256
    if mode == "score":
        acc_ref[...] = held[2][...]

    def block(n, _):
        cols = pl.ds(pl.multiple_of(n * step, step), step)
        gram = lax.dot_general(
            rows_ref[...], cols_ref[cols, :], (((1,), (1,)), ((), ())), preferred_element_type=jnp.float32
        )
        if mode == "first":
            out_ref[:, cols] = gram
        elif mode == "next":
            out_ref[:, cols] = held[0][:, cols] + gram
        else:
            both = gram * (held[0][:, cols] + held[1][:, cols])
            acc_ref[...] += jnp.sum(both.reshape(8 * CAP, rows, step), axis=1)
        return 0

    lax.fori_loop(0, SEQ_D // step, block, 0)
    if mode == "score" and not last:
        out_ref[...] = acc_ref[...]
    if last:
        total = jnp.sum(acc_ref[...], axis=1, keepdims=True)
        near = jnp.where(inner == 1, me ^ 6, me ^ 4)
        far = jnp.where(inner == 1, me ^ 4, me ^ 6)
        for k, owner in enumerate((me, me ^ 2, near, far, me ^ 1, me ^ 3, near ^ 1, far ^ 1)):
            for t in range(tensor):
                out_ref[owner * tensor + t] = jnp.broadcast_to(total[k * CAP : (k + 1) * CAP], (CAP, 128))


def gram_call(me, codes, own, came, at, arrays, offs, partner, part, far, side, doc, off, token, mode, held,
              last, tensor):
    late = arrays[-2]
    rows, width = late.shape[1:]
    tokens = doc.shape[1]
    total = 8 * CAP * rows
    args = [me, codes, own, came, *arrays, partner, far, side, doc, token]
    if last:
        out = jax.ShapeDtypeStruct((8 * tensor, CAP, 128), jnp.float32)
    elif mode == "score":
        out = jax.ShapeDtypeStruct((8 * CAP, 256), jnp.float32)
    else:
        out = jax.ShapeDtypeStruct((total, tokens), jnp.float32)
    return pl.pallas_call(
        functools.partial(gram_kernel, offs=offs, off=off, at=at, part=part, mode=mode, last=last, tensor=tensor),
        out_shape=out,
        in_specs=[SMEM, SMEM] + [ANY] * (len(args) - 2) + [VMEM] * len(held),
        out_specs=VMEM,
        scratch_shapes=[
            pltpu.VMEM((total, width), doc.dtype),
            pltpu.VMEM((tokens, width), doc.dtype),
            pltpu.VMEM((8 * CAP, 256), jnp.float32),
            pltpu.SemaphoreType.DMA((1,)),
            pltpu.SemaphoreType.DMA((5 * CAP,)),
            pltpu.SemaphoreType.DMA((3 * CAP,)),
        ],
        compiler_params=pltpu.CompilerParams(vmem_limit_bytes=16 * 1024 * 1024),
        cost_estimate=CHEAP,
    )(*args, *held)


def finish_kernel(came_ref, place_ref, out_ref, *, tensor):
    factor = 1.0 / jnp.sqrt(jnp.float32(FF) * jnp.float32(D) * jnp.float32(SEQ_S) * jnp.float32(SEQ_D))
    for p in range(8 * CAP):
        slot = place_ref[p]
        doc, r = slot // CAP, slot % CAP
        total = came_ref[doc * tensor, r, 0]
        for t in range(1, tensor):
            total = total + came_ref[doc * tensor + t, r, 0]
        out_ref[p] = total * factor


def chain(sample_act, sample_grad, doc_act, doc_grad, pair_doc, pair_sample):
    groups, tensor = lax.axis_size("groups"), lax.axis_size("tensor")
    me = jnp.stack([lax.axis_index("docs"), lax.axis_index("groups")]).astype(jnp.int32)
    chunks = [(True, 0, CHUNK), (True, CHUNK, CHUNK)]
    off = 0
    for w in WIDTHS:
        chunks.append((False, off, w))
        off += w
    chunks.append((False, off, sample_act.shape[2] - off))
    total = len(chunks)
    send = lambda x, pairs: lax.ppermute(x, "docs", pairs)
    tab, place, own, z, across = start_call(me, pair_doc, pair_sample, sample_grad, sample_act)
    z0 = send(z, OVER_Z)
    early_grad = send(across, ACROSS)
    tables = lax.all_to_all(
        jnp.broadcast_to(tab[None, :], (groups * 8, 8 * CAP)), ("groups", "docs"), 0, 0, tiled=True
    )
    codes = codes_call(me, tables, groups)
    listed = list_call(me, tab, tables, early_grad)

    def send_extras(count):
        if count == 0:
            return blank_call([(EXTRAS[-1],) + x.shape[1:] for x in (sample_grad, sample_act)], own)
        sent = [send(x, ACROSS) for x in ahead_call(count, own, sample_grad, sample_act)]
        return tuple(jnp.pad(x, ((0, EXTRAS[-1] - count), (0, 0), (0, 0))) for x in sent)

    extras = lax.switch(codes[BRANCH], [functools.partial(send_extras, c) for c in EXTRAS])

    ahead_of = [(z0, 0)]
    main, late, sides = {}, {}, {}
    state = dict(grads=None, score=None)

    def came(i):
        return ahead_of[i] if i < LEAD else (main[i - LEAD], 0)

    def partner(i):
        array, first = ahead_of[i // 2]
        return array, first + i % 2 * 2 * CAP

    def sample(i):
        return sample_grad if chunks[i][0] else sample_act

    def over_arrays(i):
        is_grad, off, _ = chunks[i]
        extra = extras[0 if is_grad else 1]
        if not is_grad:
            return [late[i], extra], (None, off)
        return [early_grad, late[i], extra], (off, off)

    def mix(i, token):
        _, off, w = chunks[i]
        first = OWN if chunks[i][0] else 0
        out = mix_call(me, listed, sample(i), *came(i), MAIN - first, first, off, w, token)
        late[i] = send(out, ACROSS)
        return out

    def forward(i, token):
        ahead = chunks[i + LEAD][1:] if i + LEAD < total else None
        out = forward_call(me, codes, *over_arrays(i), sample_act, ahead, token)
        main[i] = send(out, OVER_Z)
        return out

    def side(i, token):
        out = side_call(me, codes, tab, sample(i), *came(i), *over_arrays(i), *partner(i), main[i], chunks[i][1],
                        token)
        sides[i] = send(out, OVER_Y)
        return out

    def gram(i, token):
        is_grad, off, w = chunks[i]
        last = i == total - 1
        if is_grad:
            held = [] if i == 0 else [state["grads"]]
            mode = "next" if held else "first"
        else:
            held, mode = [*state["grads"], state["score"]], "score"
        out = gram_call(
            me, codes, sample(i), *came(i), *over_arrays(i), *partner(i), main[i], sides[i],
            doc_grad if is_grad else doc_act, off, token, mode, held, last, tensor,
        )
        if not is_grad:
            state["score"] = out
        elif chunks[i + 1][0]:
            state["grads"] = out
        else:
            state["grads"] = (out, lax.psum(out, "tensor") - out if tensor != 2 else lax.ppermute(
                out, "tensor", [(0, 1), (1, 0)]
            ))
            state["score"] = jnp.zeros((8 * CAP, 256), jnp.float32)
        return out

    token = mix(0, listed)
    spans = [c[1:] for c in chunks[2:]]

    def ahead_block(i, token):
        out = ahead_block_call(me, tab, sample_act, sample(i), token, spans[2 * i - 2 : 2 * i], chunks[i][1:])
        ahead_of.append((send(out, OVER_Z), 0))
        return out

    token = ahead_block(1, token)
    ahead_block(2, token)
    token = extras[0]
    for i in range(total + 2):
        if i + 1 < total:
            token = mix(i + 1, token)
        if i < total:
            token = forward(i, token)
        if i == 4:
            token = gram(1, token)
        if i == 0:
            token = ahead_block(3, token)
        if 1 <= i < total + 1:
            token = side(i - 1, token)
        if i >= 2 and i != 3:
            token = gram(i - 2, token)
    back = lax.all_to_all(state["score"], ("docs", "tensor"), 0, 0, tiled=True)
    return pl.pallas_call(
        functools.partial(finish_kernel, tensor=tensor),
        out_shape=jax.ShapeDtypeStruct((8 * CAP,), jnp.float32),
        in_specs=[SMEM, SMEM],
        out_specs=SMEM,
        compiler_params=SMALL,
        cost_estimate=CHEAP,
    )(back, place)


def list_kernel(me_ref, mine_ref, all_ref, token_ref, out_ref, scratch):
    me = me_ref[0]
    first = jnp.where(me < 4, 8, 0)
    mine, partner = jnp.int32(0), jnp.int32(0)
    for j in range(8):
        mine = mine | jnp.left_shift(1, mine_ref[first + j])
        partner = partner | jnp.left_shift(1, all_ref[me_ref[1] * 8 + (me ^ 2), first + j])
    for i in range(32):
        scratch[i] = 0
    for i in range(16):
        out_ref[i] = 0
    count = jnp.int32(0)
    for s in range(8):
        hit = (mine >> s) & 1
        scratch[jnp.where(hit == 1, count, 31)] = s
        count = count + hit
    count = jnp.maximum(count, OWN)
    for s in range(8):
        hit = (partner >> s) & 1
        scratch[jnp.where(hit == 1, count, 31)] = 8 + s
        count = count + hit
    need = jnp.maximum(count - MAIN, 0)
    for k in range(MAIN):
        out_ref[LIST + k] = scratch[k if k < OWN else k + need]


def list_call(me, mine, tables, token):
    return pl.pallas_call(
        list_kernel,
        out_shape=jax.ShapeDtypeStruct((16,), jnp.int32),
        in_specs=[SMEM, SMEM, SMEM, ANY],
        out_specs=SMEM,
        scratch_shapes=[pltpu.SMEM((32,), jnp.int32)],
        compiler_params=SMALL,
        cost_estimate=CHEAP,
    )(me, mine, tables, token)


def codes_kernel(me_ref, all_ref, out_ref, masks, *, groups):
    group, me = me_ref[1], me_ref[0]
    base = group * 8

    def owner_mask(row, _):
        first = jnp.where((row & 7) < 4, 8, 0)
        mask = jnp.int32(0)
        for j in range(8):
            mask = mask | jnp.left_shift(1, all_ref[row, first + j])
        masks[row] = mask
        return 0

    lax.fori_loop(0, groups * 8, owner_mask, 0)

    def longest(k, best):
        row = (k >> 2) * 8 + 2 + (k & 3)
        return jnp.maximum(best, jnp.maximum(bits(masks[row]), OWN) + bits(masks[row ^ 2]))

    best = lax.fori_loop(0, groups * 4, longest, jnp.int32(0))
    branch = jnp.int32(0)
    for c in EXTRAS[:-1]:
        branch = branch + (best > MAIN + c).astype(jnp.int32)
    for i in range(CODES):
        out_ref[i] = 0
    out_ref[BRANCH] = branch
    inner = is_inner(me)
    far, far_outer = masks[base + (me ^ 6)], masks[base + (me ^ 4)]
    after = jnp.maximum(bits(far), OWN)
    extra = jnp.maximum(after + bits(far_outer) - MAIN, 0)

    def place(near, doc, r):
        owner = base + ((me ^ 6) if near else (me ^ 4))
        sample = all_ref[owner, doc * CAP + r]
        below = jnp.left_shift(1, sample) - 1
        if near:
            at = bits(far & below)
            at = jnp.where(at < OWN, at, jnp.where(at < OWN + extra, at - OWN + SENT, at - extra))
        else:
            at = after + bits(far_outer & below) - extra
        return at * inner

    for r in range(CAP):
        out_ref[STRAIGHT + r] = place(True, me ^ 2, r)
        out_ref[STRAIGHT + CAP + r] = place(False, me ^ 2, r)
        out_ref[DIAG + r] = place(True, me ^ 3, r)
        out_ref[DIAG + CAP + r] = place(False, me ^ 3, r)
        out_ref[SIDE + r] = all_ref[base + (me ^ 2), (me ^ 1) * CAP + r]
        out_ref[SIDE + CAP + r] = place(True, me ^ 1, r)
        out_ref[SIDE + 2 * CAP + r] = place(False, me ^ 1, r)
        out_ref[SLOTS + r] = all_ref[base + me, me * CAP + r]
        out_ref[SLOTS + CAP + r] = all_ref[base + (me ^ 2), me * CAP + r]
        out_ref[SLOTS + 2 * CAP + r] = place(True, me, r)
        out_ref[SLOTS + 3 * CAP + r] = place(False, me, r)


def codes_call(me, tables, groups):
    return pl.pallas_call(
        functools.partial(codes_kernel, groups=groups),
        out_shape=jax.ShapeDtypeStruct((CODES,), jnp.int32),
        in_specs=[SMEM, SMEM],
        out_specs=SMEM,
        scratch_shapes=[pltpu.SMEM((groups * 8,), jnp.int32)],
        compiler_params=SMALL,
        cost_estimate=CHEAP,
    )(me, tables)


def direct(sample_act, sample_grad, doc_act, doc_grad, pair_doc, pair_sample):
    owners = lax.axis_size("docs")
    pair_count = pair_doc.shape[0]
    slot_count = owners * CAP
    factor = 1.0 / jnp.sqrt(
        jnp.float32(FF) * jnp.float32(D) * jnp.float32(SEQ_S) * jnp.float32(SEQ_D)
    )
    target = pair_doc[:, 0]
    order = jnp.arange(pair_count, dtype=jnp.int32)
    earlier = (target[:, None] == target[None, :]) & (order[None, :] < order[:, None])
    rank = jnp.sum(earlier.astype(jnp.int32), axis=1)
    slot_of_pair = target * CAP + rank
    chosen = (jnp.arange(slot_count, dtype=jnp.int32)[:, None] == slot_of_pair[None, :]).astype(
        jnp.int32
    )
    slot_sample = jnp.sum(chosen * pair_sample[None, :], axis=1)
    send_act = sample_act[slot_sample]
    send_grad = sample_grad[slot_sample]
    send_act = send_act.reshape(owners, CAP, send_act.shape[1], send_act.shape[2])
    send_grad = send_grad.reshape(owners, CAP, send_grad.shape[1], send_grad.shape[2])
    grad_in = lax.all_to_all(send_grad, "docs", split_axis=0, concat_axis=0, tiled=True)
    act_in = lax.all_to_all(send_act, "docs", split_axis=0, concat_axis=0, tiled=True)
    grad_gram = jnp.einsum("nmsf,tf->nmst", grad_in, doc_grad[0], preferred_element_type=jnp.float32)
    grad_sum = lax.psum(grad_gram, "tensor")
    act_gram = jnp.einsum("nmsf,tf->nmst", act_in, doc_act[0], preferred_element_type=jnp.float32)
    scores = lax.psum(jnp.sum(act_gram * grad_sum, axis=(2, 3)) * factor, "tensor")
    returned = lax.all_to_all(scores, "docs", split_axis=0, concat_axis=0, tiled=True)
    flat_scores = returned.reshape(slot_count)
    return jnp.sum(jnp.where(chosen > 0, flat_scores[:, None], 0.0), axis=0)


def solution(mesh):
    in_specs = (
        P(("groups", "docs"), None, "tensor"),
        P(("groups", "docs"), None, "tensor"),
        P(("groups", "docs"), None, "tensor"),
        P(("groups", "docs"), None, "tensor"),
        P(("groups", "docs"), None),
        P(("groups", "docs")),
    )
    out_specs = P(("groups", "docs"))

    def per_device(sample_act, sample_grad, doc_act, doc_grad, pair_doc, pair_sample):
        fits = (
            mesh.shape["docs"] == 8
            and mesh.shape["tensor"] == 2
            and pair_doc.shape[0] == 8 * CAP
            and sample_act.shape[0] == 8
            and sample_grad.shape[2] == 2 * CHUNK
            and 0 < sample_act.shape[2] - sum(WIDTHS) <= CHUNK
            and sample_act.shape[2] % 128 == 0
        )
        run = chain if fits else direct
        return run(sample_act, sample_grad, doc_act, doc_grad, pair_doc, pair_sample)

    return jax.shard_map(
        per_device, mesh=mesh, in_specs=in_specs, out_specs=out_specs, check_vma=False
    )
```

```python
import functools

import jax
import jax.numpy as jnp
from jax import lax
from jax.experimental import pallas as pl
from jax.experimental.pallas import tpu as pltpu
from jax.sharding import PartitionSpec as P

FF = 11008
D = 4096
SEQ_S = 32
SEQ_D = 768
CAP = 2

ANY = pl.BlockSpec(memory_space=pl.ANY)
SMEM = pl.BlockSpec(memory_space=pltpu.SMEM)
VMEM = pl.BlockSpec(memory_space=pltpu.VMEM)

INNER = (2, 3, 4, 5)
ACROSS = [(i, i ^ 6) for i in INNER]
OVER_Z = [(i, i ^ 2) for i in range(8)]
OVER_Y = [(i, i ^ 1) for i in range(8)]

OWN = 4
MAIN = 12
EXTRAS = (0, 1, 2, 4)

LIST, STRAIGHT, DIAG, SIDE, SLOTS, BRANCH, CODES = 0, 16, 20, 24, 32, 48, 64
SENT = 16


def is_inner(me):
    return ((me >> 1) ^ (me >> 2)) & 1


def bits(mask):
    total = mask & 1
    for i in range(1, 8):
        total = total + ((mask >> i) & 1)
    return total


SMALL = pltpu.CompilerParams(vmem_limit_bytes=6 * 1024 * 1024)
CHEAP = pl.CostEstimate(flops=0, bytes_accessed=1024, transcendentals=0)
CHUNK = 1024
WIDTHS = (1024, 1024, 1024, 1024, 768)
LEAD = 4


class Copies:
    def __init__(self, sems):
        self.sems, self.used, self.held = sems, 0, []

    def start(self, src, dst):
        copy = pltpu.make_async_copy(src, dst, self.sems.at[self.used])
        copy.start()
        self.used += 1
        self.held.append(copy)

    def either(self, first, src, other, dst):
        sem = self.sems.at[self.used]

        @pl.when(first)
        def _():
            pltpu.make_async_copy(src, dst, sem).start()

        @pl.when(jnp.logical_not(first))
        def _():
            pltpu.make_async_copy(other, dst, sem).start()

        self.used += 1
        self.held.append(pltpu.make_async_copy(src, dst, sem))

    def wait(self):
        for copy in self.held:
            copy.wait()
        self.held = []


def cut(ref, i, off, width):
    return ref.at[i, :, pl.ds(off, width)]


def own_slots(sems, inner, me, tab_ref, here, ahead, dst, first):
    @pl.when(inner == 1)
    def _():
        c = Copies(sems)
        for part, (ref, off, width) in enumerate(here):
            for k in range(2 * CAP):
                sample = tab_ref[(me ^ (2 + k // CAP)) * CAP + k % CAP]
                c.start(cut(ref, sample, off, width), cut(dst, first + part * 2 * CAP + k, 0, width))
        c.wait()

    @pl.when(inner == 0)
    def _():
        c = Copies(sems)
        ref, off, width = ahead
        for s in range(8):
            c.start(cut(ref, s, off, width), cut(dst, first + s, 0, width))
        c.wait()


def start_kernel(me_ref, doc_ref, sample_ref, grad_ref, act_ref, tab_ref, place_ref, own_ref, z_ref, across_ref,
                 seen, sems, out_sems):
    me = me_ref[0]
    inner = is_inner(me)
    for d in range(8):
        seen[d] = 0
    for i in range(8 * CAP):
        tab_ref[i] = 0
    for i in range(16):
        own_ref[i] = 0
    mask = jnp.int32(0)
    half = me >> 2
    for p in range(8 * CAP):
        doc = doc_ref[p, 0]
        slot = doc * CAP + jnp.minimum(seen[doc], CAP - 1)
        seen[doc] = seen[doc] + 1
        place_ref[p] = slot
        tab_ref[slot] = sample_ref[p]
        bit = jnp.left_shift(1, sample_ref[p])
        mask = jnp.where((doc >> 2) != half, mask | bit, mask)
    count = jnp.int32(0)
    for s in range(8):
        hit = (mask >> s) & 1
        own_ref[jnp.where(hit == 1, count, 8)] = s
        count = count + hit
    width = grad_ref.shape[2] // 2
    lists = Copies(sems)
    for k in range(OWN):
        lists.start(cut(grad_ref, own_ref[k], 0, 2 * width), across_ref.at[k])
    own_slots(out_sems, inner, me, tab_ref,
              ((grad_ref, 0, width), (grad_ref, width, width)), (grad_ref, 0, width), z_ref, 0)
    lists.wait()


def start_call(me, pair_doc, pair_sample, grad, act):
    rows, width = grad.shape[1:]
    table = jax.ShapeDtypeStruct((16,), jnp.int32)
    return pl.pallas_call(
        start_kernel,
        out_shape=(table, table, table, jax.ShapeDtypeStruct((8, rows, CHUNK), grad.dtype),
                   jax.ShapeDtypeStruct((OWN, rows, width), grad.dtype)),
        in_specs=[SMEM, SMEM, SMEM, ANY, ANY],
        out_specs=(SMEM, SMEM, SMEM, VMEM, VMEM),
        scratch_shapes=[pltpu.SMEM((8,), jnp.int32), pltpu.SemaphoreType.DMA((OWN,)),
                        pltpu.SemaphoreType.DMA((8,))],
        compiler_params=SMALL,
        cost_estimate=CHEAP,
    )(me, pair_doc, pair_sample, grad, act)


def ahead_block_kernel(me_ref, tab_ref, act_ref, far_ref, token_ref, z_ref, sems, *, here, ahead):
    me = me_ref[0]
    own_slots(sems, is_inner(me), me, tab_ref, [(act_ref, *span) for span in here], (far_ref, *ahead), z_ref, 0)


def ahead_block_call(me, tab, act, far, token, here, ahead):
    return pl.pallas_call(
        functools.partial(ahead_block_kernel, here=here, ahead=ahead),
        out_shape=jax.ShapeDtypeStruct((8, act.shape[1], CHUNK), act.dtype),
        in_specs=[SMEM, SMEM, ANY, ANY, ANY],
        out_specs=VMEM,
        scratch_shapes=[pltpu.SemaphoreType.DMA((8,))],
        compiler_params=SMALL,
        cost_estimate=CHEAP,
    )(me, tab, act, far, token)


def mix_kernel(me_ref, codes_ref, own_ref, came_ref, token_ref, list_ref, sems, *, first, off, at):
    count, _, width = list_ref.shape

    @pl.when(is_inner(me_ref[0]) == 1)
    def _():
        copies = Copies(sems)
        for k in range(count):
            code = codes_ref[LIST + first + k]
            mine = code < 8
            copies.either(mine, cut(own_ref, jnp.minimum(code, 7), off, width),
                          cut(came_ref, at + jnp.maximum(code - 8, 0), 0, width), list_ref.at[k])
        copies.wait()


def mix_call(me, codes, own, came, at, count, first, off, width, token):
    rows = own.shape[1]
    return pl.pallas_call(
        functools.partial(mix_kernel, first=first, off=off, at=at),
        out_shape=jax.ShapeDtypeStruct((count, rows, width), own.dtype),
        in_specs=[SMEM, SMEM, ANY, ANY, ANY],
        out_specs=VMEM,
        scratch_shapes=[pltpu.SemaphoreType.DMA((count,))],
        compiler_params=SMALL,
        cost_estimate=CHEAP,
    )(me, codes, own, came, token)


def entry(copies, code, came_over, width, dst):
    early, late_ref, (extra_ref, extra_off) = came_over
    sem = copies.sems.at[copies.used]
    copies.used += 1
    skip = 0 if early is None else OWN

    @pl.when(code >= SENT)
    def _():
        pltpu.make_async_copy(cut(extra_ref, jnp.maximum(code - SENT, 0), extra_off, width), dst, sem).start()

    @pl.when((code >= skip) & (code < SENT))
    def _():
        at = jnp.clip(code - skip, 0, late_ref.shape[0] - 1)
        pltpu.make_async_copy(cut(late_ref, at, 0, width), dst, sem).start()

    if early is not None:
        @pl.when(code < OWN)
        def _():
            pltpu.make_async_copy(cut(early[0], jnp.minimum(code, OWN - 1), early[1], width), dst, sem).start()

    copies.held.append(pltpu.make_async_copy(cut(late_ref, 0, 0, width), dst, sem))


def over(rest, early_off, extra_off):
    early = None if early_off is None else (rest.pop(0), early_off)
    return early, rest.pop(0), (rest.pop(0), extra_off)


def blank_kernel(token_ref, *refs):
    pass


def blank_call(shapes, token):
    return tuple(pl.pallas_call(
        blank_kernel,
        out_shape=[jax.ShapeDtypeStruct(x, jnp.bfloat16) for x in shapes],
        in_specs=[SMEM],
        out_specs=[ANY] * len(shapes),
        compiler_params=SMALL,
        cost_estimate=CHEAP,
    )(token))


def ahead_kernel(own_ref, grad_ref, act_ref, grad_out, act_out, sems):
    copies = Copies(sems)
    for k in range(grad_out.shape[0]):
        copies.start(grad_ref.at[own_ref[OWN + k]], grad_out.at[k])
        copies.start(act_ref.at[own_ref[OWN + k]], act_out.at[k])
    copies.wait()


def ahead_call(count, own, grad, act):
    return pl.pallas_call(
        ahead_kernel,
        out_shape=tuple(jax.ShapeDtypeStruct((count,) + x.shape[1:], x.dtype) for x in (grad, act)),
        in_specs=[SMEM, ANY, ANY],
        out_specs=(VMEM, VMEM),
        scratch_shapes=[pltpu.SemaphoreType.DMA((2 * count,))],
        compiler_params=SMALL,
        cost_estimate=CHEAP,
    )(own, grad, act)


def forward_kernel(me_ref, codes_ref, *rest, offs, ahead):
    rest = list(rest)
    came_over = over(rest, *offs)
    ahead_ref, token_ref, z_ref, sems = rest
    inner = is_inner(me_ref[0])
    width = came_over[1].shape[2]

    @pl.when(inner == 1)
    def _():
        copies = Copies(sems)
        for k in range(2 * CAP):
            entry(copies, codes_ref[STRAIGHT + k], came_over, width, cut(z_ref, k, 0, width))
            entry(copies, codes_ref[DIAG + k], came_over, width, cut(z_ref, 2 * CAP + k, 0, width))
        copies.wait()

    if ahead is not None:
        @pl.when(inner == 0)
        def _():
            copies = Copies(sems)
            off, some = ahead
            for s in range(8):
                copies.start(cut(ahead_ref, s, off, some), cut(z_ref, s, 0, some))
            copies.wait()


def forward_call(me, codes, arrays, offs, ahead_array, ahead, token):
    late = arrays[-2]
    rows, width = late.shape[1:]
    args = [me, codes, *arrays, ahead_array, token]
    return pl.pallas_call(
        functools.partial(forward_kernel, offs=offs, ahead=ahead),
        out_shape=jax.ShapeDtypeStruct((8, rows, width), late.dtype),
        in_specs=[SMEM, SMEM] + [ANY] * (len(args) - 2),
        out_specs=VMEM,
        scratch_shapes=[pltpu.SemaphoreType.DMA((8,))],
        compiler_params=SMALL,
        cost_estimate=CHEAP,
    )(*args)


def side_kernel(me_ref, codes_ref, tab_ref, sample_ref, came_ref, *rest, offs, off, at, part):
    rest = list(rest)
    came_over = over(rest, *offs)
    own_ref, far_ref, token_ref, side_ref, sems, role_sems = rest
    me = me_ref[0]
    inner = is_inner(me)
    width = side_ref.shape[2]
    mine = Copies(sems)
    for r in range(CAP):
        mine.start(cut(sample_ref, tab_ref[(me ^ 1) * CAP + r], off, width), side_ref.at[r])

    @pl.when(inner == 1)
    def _():
        copies = Copies(role_sems)
        for k in range(CAP):
            copies.start(cut(came_ref, at + codes_ref[SIDE + k], 0, width), side_ref.at[CAP + k])
        for k in range(CAP, 3 * CAP):
            entry(copies, codes_ref[SIDE + k], came_over, width, side_ref.at[CAP + k])
        copies.wait()

    @pl.when(inner == 0)
    def _():
        copies = Copies(role_sems)
        for k in range(CAP):
            copies.start(cut(own_ref, part + CAP + k, 0, width), side_ref.at[CAP + k])
        for k in range(2 * CAP):
            copies.start(cut(far_ref, 2 * CAP + k, 0, width), side_ref.at[2 * CAP + k])
        copies.wait()

    mine.wait()


def side_call(me, codes, tab, sample, came, at, arrays, offs, own, part, far, off, token):
    late = arrays[-2]
    rows, width = late.shape[1:]
    args = [me, codes, tab, sample, came, *arrays, own, far, token]
    return pl.pallas_call(
        functools.partial(side_kernel, offs=offs, off=off, at=at, part=part),
        out_shape=jax.ShapeDtypeStruct((4 * CAP, rows, width), late.dtype),
        in_specs=[SMEM, SMEM, SMEM] + [ANY] * (len(args) - 3),
        out_specs=VMEM,
        scratch_shapes=[pltpu.SemaphoreType.DMA((CAP,)), pltpu.SemaphoreType.DMA((3 * CAP,))],
        compiler_params=SMALL,
        cost_estimate=CHEAP,
    )(*args)


def gram_kernel(me_ref, codes_ref, own_ref, came_ref, *rest, offs, off, at, part, mode, last, tensor):
    rest = list(rest)
    came_over = over(rest, *offs)
    partner_ref, far_ref, side_ref, doc_ref, token_ref = rest[:5]
    rest = rest[5:]
    held = [rest.pop(0) for _ in range({"first": 0, "next": 1, "score": 3}[mode])]
    out_ref, rows_ref, cols_ref, acc_ref, doc_sem, sems, role_sems = rest
    me = me_ref[0]
    inner = is_inner(me)
    rows = own_ref.shape[1]
    width = rows_ref.shape[1]
    docs = pltpu.make_async_copy(doc_ref.at[0, :, pl.ds(off, width)], cols_ref, doc_sem.at[0])
    docs.start()

    def slot(k):
        return rows_ref.at[pl.ds(k * rows, rows), :]

    copies = Copies(sems)
    for r in range(CAP):
        copies.start(cut(own_ref, codes_ref[SLOTS + r], off, width), slot(r))
    for k in range(4 * CAP):
        copies.start(side_ref.at[k], slot(4 * CAP + k))

    @pl.when(inner == 1)
    def _():
        more = Copies(role_sems)
        for r in range(CAP):
            more.start(cut(came_ref, at + codes_ref[SLOTS + CAP + r], 0, width), slot(CAP + r))
        for k in range(2 * CAP, 4 * CAP):
            entry(more, codes_ref[SLOTS + k], came_over, width, slot(k))
        more.wait()

    @pl.when(inner == 0)
    def _():
        more = Copies(role_sems)
        for r in range(CAP):
            more.start(cut(partner_ref, part + r, 0, width), slot(CAP + r))
        for k in range(2 * CAP):
            more.start(cut(far_ref, k, 0, width), slot(2 * CAP + k))
        more.wait()

    copies.wait()
    docs.wait()
    step = 256
    if mode == "score":
        acc_ref[...] = held[2][...]

    def block(n, _):
        cols = pl.ds(pl.multiple_of(n * step, step), step)
        gram = lax.dot_general(
            rows_ref[...], cols_ref[cols, :], (((1,), (1,)), ((), ())), preferred_element_type=jnp.float32
        )
        if mode == "first":
            out_ref[:, cols] = gram
        elif mode == "next":
            out_ref[:, cols] = held[0][:, cols] + gram
        else:
            both = gram * (held[0][:, cols] + held[1][:, cols])
            acc_ref[...] += jnp.sum(both.reshape(8 * CAP, rows, step), axis=1)
        return 0

    lax.fori_loop(0, SEQ_D // step, block, 0)
    if mode == "score" and not last:
        out_ref[...] = acc_ref[...]
    if last:
        total = jnp.sum(acc_ref[...], axis=1, keepdims=True)
        near = jnp.where(inner == 1, me ^ 6, me ^ 4)
        far = jnp.where(inner == 1, me ^ 4, me ^ 6)
        for k, owner in enumerate((me, me ^ 2, near, far, me ^ 1, me ^ 3, near ^ 1, far ^ 1)):
            for t in range(tensor):
                out_ref[owner * tensor + t] = jnp.broadcast_to(total[k * CAP : (k + 1) * CAP], (CAP, 128))


def gram_call(me, codes, own, came, at, arrays, offs, partner, part, far, side, doc, off, token, mode, held,
              last, tensor):
    late = arrays[-2]
    rows, width = late.shape[1:]
    tokens = doc.shape[1]
    total = 8 * CAP * rows
    args = [me, codes, own, came, *arrays, partner, far, side, doc, token]
    if last:
        out = jax.ShapeDtypeStruct((8 * tensor, CAP, 128), jnp.float32)
    elif mode == "score":
        out = jax.ShapeDtypeStruct((8 * CAP, 256), jnp.float32)
    else:
        out = jax.ShapeDtypeStruct((total, tokens), jnp.float32)
    return pl.pallas_call(
        functools.partial(gram_kernel, offs=offs, off=off, at=at, part=part, mode=mode, last=last, tensor=tensor),
        out_shape=out,
        in_specs=[SMEM, SMEM] + [ANY] * (len(args) - 2) + [VMEM] * len(held),
        out_specs=VMEM,
        scratch_shapes=[
            pltpu.VMEM((total, width), doc.dtype),
            pltpu.VMEM((tokens, width), doc.dtype),
            pltpu.VMEM((8 * CAP, 256), jnp.float32),
            pltpu.SemaphoreType.DMA((1,)),
            pltpu.SemaphoreType.DMA((5 * CAP,)),
            pltpu.SemaphoreType.DMA((3 * CAP,)),
        ],
        compiler_params=pltpu.CompilerParams(vmem_limit_bytes=16 * 1024 * 1024),
        cost_estimate=CHEAP,
    )(*args, *held)


def finish_kernel(came_ref, place_ref, out_ref, *, tensor):
    factor = 1.0 / jnp.sqrt(jnp.float32(FF) * jnp.float32(D) * jnp.float32(SEQ_S) * jnp.float32(SEQ_D))
    for p in range(8 * CAP):
        slot = place_ref[p]
        doc, r = slot // CAP, slot % CAP
        total = came_ref[doc * tensor, r, 0]
        for t in range(1, tensor):
            total = total + came_ref[doc * tensor + t, r, 0]
        out_ref[p] = total * factor


def chain(sample_act, sample_grad, doc_act, doc_grad, pair_doc, pair_sample):
    groups, tensor = lax.axis_size("groups"), lax.axis_size("tensor")
    me = jnp.stack([lax.axis_index("docs"), lax.axis_index("groups")]).astype(jnp.int32)
    chunks = [(True, 0, CHUNK), (True, CHUNK, CHUNK)]
    off = 0
    for w in WIDTHS:
        chunks.append((False, off, w))
        off += w
    chunks.append((False, off, sample_act.shape[2] - off))
    total = len(chunks)
    send = lambda x, pairs: lax.ppermute(x, "docs", pairs)
    tab, place, own, z, across = start_call(me, pair_doc, pair_sample, sample_grad, sample_act)
    z0 = send(z, OVER_Z)
    early_grad = send(across, ACROSS)
    tables = lax.all_to_all(
        jnp.broadcast_to(tab[None, :], (groups * 8, 8 * CAP)), ("groups", "docs"), 0, 0, tiled=True
    )
    codes = codes_call(me, tables, groups)
    listed = list_call(me, tab, tables, early_grad)

    def send_extras(count):
        if count == 0:
            return blank_call([(EXTRAS[-1],) + x.shape[1:] for x in (sample_grad, sample_act)], own)
        sent = [send(x, ACROSS) for x in ahead_call(count, own, sample_grad, sample_act)]
        return tuple(jnp.pad(x, ((0, EXTRAS[-1] - count), (0, 0), (0, 0))) for x in sent)

    extras = lax.switch(codes[BRANCH], [functools.partial(send_extras, c) for c in EXTRAS])

    ahead_of = [(z0, 0)]
    main, late, sides = {}, {}, {}
    state = dict(grads=None, score=None)

    def came(i):
        return ahead_of[i] if i < LEAD else (main[i - LEAD], 0)

    def partner(i):
        array, first = ahead_of[i // 2]
        return array, first + i % 2 * 2 * CAP

    def sample(i):
        return sample_grad if chunks[i][0] else sample_act

    def over_arrays(i):
        is_grad, off, _ = chunks[i]
        extra = extras[0 if is_grad else 1]
        if not is_grad:
            return [late[i], extra], (None, off)
        return [early_grad, late[i], extra], (off, off)

    def mix(i, token):
        _, off, w = chunks[i]
        first = OWN if chunks[i][0] else 0
        out = mix_call(me, listed, sample(i), *came(i), MAIN - first, first, off, w, token)
        late[i] = send(out, ACROSS)
        return out

    def forward(i, token):
        ahead = chunks[i + LEAD][1:] if i + LEAD < total else None
        out = forward_call(me, codes, *over_arrays(i), sample_act, ahead, token)
        main[i] = send(out, OVER_Z)
        return out

    def side(i, token):
        out = side_call(me, codes, tab, sample(i), *came(i), *over_arrays(i), *partner(i), main[i], chunks[i][1],
                        token)
        sides[i] = send(out, OVER_Y)
        return out

    def gram(i, token):
        is_grad, off, w = chunks[i]
        last = i == total - 1
        if is_grad:
            held = [] if i == 0 else [state["grads"]]
            mode = "next" if held else "first"
        else:
            held, mode = [*state["grads"], state["score"]], "score"
        out = gram_call(
            me, codes, sample(i), *came(i), *over_arrays(i), *partner(i), main[i], sides[i],
            doc_grad if is_grad else doc_act, off, token, mode, held, last, tensor,
        )
        if not is_grad:
            state["score"] = out
        elif chunks[i + 1][0]:
            state["grads"] = out
        else:
            state["grads"] = (out, lax.psum(out, "tensor") - out if tensor != 2 else lax.ppermute(
                out, "tensor", [(0, 1), (1, 0)]
            ))
            state["score"] = jnp.zeros((8 * CAP, 256), jnp.float32)
        return out

    token = mix(0, listed)
    spans = [c[1:] for c in chunks[2:]]

    def ahead_block(i, token):
        out = ahead_block_call(me, tab, sample_act, sample(i), token, spans[2 * i - 2 : 2 * i], chunks[i][1:])
        ahead_of.append((send(out, OVER_Z), 0))
        return out

    token = ahead_block(1, token)
    ahead_block(2, token)
    token = extras[0]
    for i in range(total + 2):
        if i + 1 < total:
            token = mix(i + 1, token)
        if i < total:
            token = forward(i, token)
        if i == 0:
            token = ahead_block(3, token)
        if 1 <= i < total + 1:
            token = side(i - 1, token)
        if i == 4:
            token = gram(1, token)
        if i >= 2 and i != 3:
            token = gram(i - 2, token)
    back = lax.all_to_all(state["score"], ("docs", "tensor"), 0, 0, tiled=True)
    return pl.pallas_call(
        functools.partial(finish_kernel, tensor=tensor),
        out_shape=jax.ShapeDtypeStruct((8 * CAP,), jnp.float32),
        in_specs=[SMEM, SMEM],
        out_specs=SMEM,
        compiler_params=SMALL,
        cost_estimate=CHEAP,
    )(back, place)


def list_kernel(me_ref, mine_ref, all_ref, token_ref, out_ref, scratch):
    me = me_ref[0]
    first = jnp.where(me < 4, 8, 0)
    mine, partner = jnp.int32(0), jnp.int32(0)
    for j in range(8):
        mine = mine | jnp.left_shift(1, mine_ref[first + j])
        partner = partner | jnp.left_shift(1, all_ref[me_ref[1] * 8 + (me ^ 2), first + j])
    for i in range(32):
        scratch[i] = 0
    for i in range(16):
        out_ref[i] = 0
    count = jnp.int32(0)
    for s in range(8):
        hit = (mine >> s) & 1
        scratch[jnp.where(hit == 1, count, 31)] = s
        count = count + hit
    count = jnp.maximum(count, OWN)
    for s in range(8):
        hit = (partner >> s) & 1
        scratch[jnp.where(hit == 1, count, 31)] = 8 + s
        count = count + hit
    need = jnp.maximum(count - MAIN, 0)
    for k in range(MAIN):
        out_ref[LIST + k] = scratch[k if k < OWN else k + need]


def list_call(me, mine, tables, token):
    return pl.pallas_call(
        list_kernel,
        out_shape=jax.ShapeDtypeStruct((16,), jnp.int32),
        in_specs=[SMEM, SMEM, SMEM, ANY],
        out_specs=SMEM,
        scratch_shapes=[pltpu.SMEM((32,), jnp.int32)],
        compiler_params=SMALL,
        cost_estimate=CHEAP,
    )(me, mine, tables, token)


def codes_kernel(me_ref, all_ref, out_ref, masks, *, groups):
    group, me = me_ref[1], me_ref[0]
    base = group * 8

    def owner_mask(row, _):
        first = jnp.where((row & 7) < 4, 8, 0)
        mask = jnp.int32(0)
        for j in range(8):
            mask = mask | jnp.left_shift(1, all_ref[row, first + j])
        masks[row] = mask
        return 0

    lax.fori_loop(0, groups * 8, owner_mask, 0)

    def longest(k, best):
        row = (k >> 2) * 8 + 2 + (k & 3)
        return jnp.maximum(best, jnp.maximum(bits(masks[row]), OWN) + bits(masks[row ^ 2]))

    best = lax.fori_loop(0, groups * 4, longest, jnp.int32(0))
    branch = jnp.int32(0)
    for c in EXTRAS[:-1]:
        branch = branch + (best > MAIN + c).astype(jnp.int32)
    for i in range(CODES):
        out_ref[i] = 0
    out_ref[BRANCH] = branch
    inner = is_inner(me)
    far, far_outer = masks[base + (me ^ 6)], masks[base + (me ^ 4)]
    after = jnp.maximum(bits(far), OWN)
    extra = jnp.maximum(after + bits(far_outer) - MAIN, 0)

    def place(near, doc, r):
        owner = base + ((me ^ 6) if near else (me ^ 4))
        sample = all_ref[owner, doc * CAP + r]
        below = jnp.left_shift(1, sample) - 1
        if near:
            at = bits(far & below)
            at = jnp.where(at < OWN, at, jnp.where(at < OWN + extra, at - OWN + SENT, at - extra))
        else:
            at = after + bits(far_outer & below) - extra
        return at * inner

    for r in range(CAP):
        out_ref[STRAIGHT + r] = place(True, me ^ 2, r)
        out_ref[STRAIGHT + CAP + r] = place(False, me ^ 2, r)
        out_ref[DIAG + r] = place(True, me ^ 3, r)
        out_ref[DIAG + CAP + r] = place(False, me ^ 3, r)
        out_ref[SIDE + r] = all_ref[base + (me ^ 2), (me ^ 1) * CAP + r]
        out_ref[SIDE + CAP + r] = place(True, me ^ 1, r)
        out_ref[SIDE + 2 * CAP + r] = place(False, me ^ 1, r)
        out_ref[SLOTS + r] = all_ref[base + me, me * CAP + r]
        out_ref[SLOTS + CAP + r] = all_ref[base + (me ^ 2), me * CAP + r]
        out_ref[SLOTS + 2 * CAP + r] = place(True, me, r)
        out_ref[SLOTS + 3 * CAP + r] = place(False, me, r)


def codes_call(me, tables, groups):
    return pl.pallas_call(
        functools.partial(codes_kernel, groups=groups),
        out_shape=jax.ShapeDtypeStruct((CODES,), jnp.int32),
        in_specs=[SMEM, SMEM],
        out_specs=SMEM,
        scratch_shapes=[pltpu.SMEM((groups * 8,), jnp.int32)],
        compiler_params=SMALL,
        cost_estimate=CHEAP,
    )(me, tables)


def direct(sample_act, sample_grad, doc_act, doc_grad, pair_doc, pair_sample):
    owners = lax.axis_size("docs")
    pair_count = pair_doc.shape[0]
    slot_count = owners * CAP
    factor = 1.0 / jnp.sqrt(
        jnp.float32(FF) * jnp.float32(D) * jnp.float32(SEQ_S) * jnp.float32(SEQ_D)
    )
    target = pair_doc[:, 0]
    order = jnp.arange(pair_count, dtype=jnp.int32)
    earlier = (target[:, None] == target[None, :]) & (order[None, :] < order[:, None])
    rank = jnp.sum(earlier.astype(jnp.int32), axis=1)
    slot_of_pair = target * CAP + rank
    chosen = (jnp.arange(slot_count, dtype=jnp.int32)[:, None] == slot_of_pair[None, :]).astype(
        jnp.int32
    )
    slot_sample = jnp.sum(chosen * pair_sample[None, :], axis=1)
    send_act = sample_act[slot_sample]
    send_grad = sample_grad[slot_sample]
    send_act = send_act.reshape(owners, CAP, send_act.shape[1], send_act.shape[2])
    send_grad = send_grad.reshape(owners, CAP, send_grad.shape[1], send_grad.shape[2])
    grad_in = lax.all_to_all(send_grad, "docs", split_axis=0, concat_axis=0, tiled=True)
    act_in = lax.all_to_all(send_act, "docs", split_axis=0, concat_axis=0, tiled=True)
    grad_gram = jnp.einsum("nmsf,tf->nmst", grad_in, doc_grad[0], preferred_element_type=jnp.float32)
    grad_sum = lax.psum(grad_gram, "tensor")
    act_gram = jnp.einsum("nmsf,tf->nmst", act_in, doc_act[0], preferred_element_type=jnp.float32)
    scores = lax.psum(jnp.sum(act_gram * grad_sum, axis=(2, 3)) * factor, "tensor")
    returned = lax.all_to_all(scores, "docs", split_axis=0, concat_axis=0, tiled=True)
    flat_scores = returned.reshape(slot_count)
    return jnp.sum(jnp.where(chosen > 0, flat_scores[:, None], 0.0), axis=0)


def solution(mesh):
    in_specs = (
        P(("groups", "docs"), None, "tensor"),
        P(("groups", "docs"), None, "tensor"),
        P(("groups", "docs"), None, "tensor"),
        P(("groups", "docs"), None, "tensor"),
        P(("groups", "docs"), None),
        P(("groups", "docs")),
    )
    out_specs = P(("groups", "docs"))

    def per_device(sample_act, sample_grad, doc_act, doc_grad, pair_doc, pair_sample):
        fits = (
            mesh.shape["docs"] == 8
            and mesh.shape["tensor"] == 2
            and pair_doc.shape[0] == 8 * CAP
            and sample_act.shape[0] == 8
            and sample_grad.shape[2] == 2 * CHUNK
            and 0 < sample_act.shape[2] - sum(WIDTHS) <= CHUNK
            and sample_act.shape[2] % 128 == 0
        )
        run = chain if fits else direct
        return run(sample_act, sample_grad, doc_act, doc_grad, pair_doc, pair_sample)

    return jax.shard_map(
        per_device, mesh=mesh, in_specs=in_specs, out_specs=out_specs, check_vma=False
    )
```
